256 devices in a mesh: ctx: 32 (over z_lo, x, y), tp: 8 (over z_hi, core).
Axes of the slice: x: 4, y: 4, z: 8 (z_hi: 4, z_lo: 2; z = z_hi * 2 + z_lo), core: 2. Of those that a mesh axis runs over, the one named last changes fastest.
Arguments:
- residual: bfloat16 [8192, 8192], P('ctx', 'tp'), may hold values from -6 to 6
- streams: bfloat16 [8192, 3, 4096], P('ctx', None, 'tp'), may hold values from -6 to 6
- short_filter: bfloat16 [7, 3, 4096], P(None, None, 'tp'), may hold values from -2 to 2
- medium_filter: bfloat16 [128, 256], P(None, 'tp'), may hold values from -0.5 to 0.5
- queries: bfloat16 [8192, 4096], P('ctx', 'tp'), may hold values from -150 to 150
- keys: bfloat16 [8192, 4096], P('ctx', 'tp'), may hold values from -5 to 5
- values: bfloat16 [8192, 4096], P('ctx', 'tp'), may hold values from -6 to 6
- lengths: int32 [8], replicated, may hold values from 1 to 4352, 8192 in all
- w_out: bfloat16 [4096, 8192], P('tp'), may hold values from -0.125 to 0.125
Outputs:
- hyena_mix: bfloat16 [8192, 4096], P('ctx', 'tp')
- attended: bfloat16 [8192, 4096], P('ctx', 'tp')
- mixed: bfloat16 [8192, 8192], P('ctx', 'tp')
The draws below stay inside these ranges and needn't reach their ends.
Inputs may be any that keep to these rules, and one draw needn't show every extreme that they name: `lengths`: each genome has at least one base, they cover the pack, and one genome has exactly 4352 bases.
All inputs are finite; a program needn't handle non-finite values.
Results may differ from the reference program's by a relative error of at most 0.012.
Values may be sent and summed in bfloat16 or wider, within the bound.
A program may use at most 192 MiB of HBM per device.

```python
import math
import jax
import jax.numpy as jnp
import numpy as np
from jax import lax

D = 8192
HC = 4096
SHORT = 7
MEDIUM = 128
HEADS = 32
HD = 128
GENOMES = 8
TOKENS = 8192
MOST = 4352
GROUPS = 256
AC = 4096


def shared_keys(key):
    return jnp.clip(jax.random.normal(jax.random.fold_in(key, 11), (TOKENS, AC), jnp.float32), -5.0, 5.0)


def draw_keys(key, part):
    base = shared_keys(key)
    return base.astype(jnp.bfloat16)


def draw_queries(key, part):
    key = jax.random.fold_in(key, 22)
    fresh = 2.0 * jnp.clip(jax.random.normal(key, (TOKENS, AC), jnp.float32), -5.0, 5.0)
    return fresh.astype(jnp.bfloat16)


def with_spikes(entries, rng, source, target, blocks, factor):
    owner, partner = [(jnp.arange(entries.shape[dim]) // (entries.shape[dim] // blocks)).reshape([-1 if axis == dim else 1 for axis in range(entries.ndim)]) for dim in (source, target)]
    chosen = jax.random.permutation(rng, blocks)[partner]
    strong = (owner == chosen) | (owner == (partner + blocks // 2) % blocks)
    return jnp.where(strong, factor * entries, entries)


def block_levels(stream_key, extent, pieces, low, high):
    loudness = 1.0
    for position, blocks in pieces:
        steps = jax.random.uniform(jax.random.fold_in(jax.random.fold_in(stream_key, 6), position), (blocks,), jnp.float32, low / len(pieces), high / len(pieces))
        loudness = loudness * jnp.repeat(jnp.exp(steps), extent[position] // blocks).reshape((-1,) + (1,) * (len(extent) - 1 - position))
    return loudness


def split_up(number_of, total, limit, skew):
    portions = [(1 << 20) // math.isqrt(rank ** skew) + 1 for rank in range(2, number_of + 1)]
    surplus, holding = total - limit - (number_of - 1), [1] * (number_of - 1)
    while surplus > 0:
        candidates = [i for i in range(number_of - 1) if holding[i] < limit]
        pool, left = sum([portions[i] for i in candidates]), surplus
        for i in candidates:
            more = min(limit - holding[i], max(1, left * portions[i] // pool), surplus)
            holding[i] = holding[i] + more
            surplus = surplus - more
    return np.array([limit] + holding)


def uneven(rng, number_of, total, reach, slope):
    if number_of == 2:
        one = jax.random.randint(rng, (), max(1, total - reach), min(reach, total - 1) + 1)
        return jnp.stack([one, total - one])
    sizes = jnp.asarray(split_up(number_of, total, reach, slope), jnp.int32)
    twos = (number_of - 1) // 2
    source_of, sink = sizes[1:1 + 2 * twos:2], sizes[2:2 + 2 * twos:2]
    room = jnp.minimum(source_of - 1, reach - sink)
    shifted = jax.random.randint(jax.random.fold_in(rng, 1), (twos,), 0, 1 << 20) % (room + 1)
    sizes = sizes.at[1:1 + 2 * twos:2].set(source_of - shifted).at[2:2 + 2 * twos:2].set(sink + shifted)
    return sizes[jax.random.permutation(jax.random.fold_in(rng, 2), number_of)]


def centred(key, dims, scale, most, shards=(), held_as=jnp.bfloat16):
    values = scale * jax.random.normal(key, dims, jnp.float32)
    if shards:
        values = values * block_levels(key, dims, shards, -0.22, 0.18)
    return jnp.clip(values, -most, most).astype(held_as)


def noise_with(key, dims, scale, reach, pieces, heavy, held_as=jnp.bfloat16):
    array = scale * jax.random.normal(key, dims, jnp.float32)
    if pieces:
        array = array * block_levels(key, dims, pieces, -0.22, 0.18)
    return jnp.clip(with_spikes(array, jax.random.fold_in(key, 3), *heavy), -reach, reach).astype(held_as)


def setup_inputs(seed: int = 0) -> dict:
    seeds = jax.random.split(jax.random.key(seed), 10)
    residual = centred(seeds[0], (TOKENS, D), 1.0, 6.0, ((0, 32), (1, 8)))
    streams = centred(seeds[1], (TOKENS, 3, HC), 1.0, 6.0, ((0, 32), (2, 8)))
    short_filter = centred(seeds[2], (SHORT, 3, HC), SHORT ** -0.5, 2.0, ((2, 8),))
    medium_filter = centred(seeds[3], (MEDIUM, GROUPS), MEDIUM ** -0.5, 0.5, ((1, 8),))
    queries = draw_queries(jax.random.fold_in(seeds[9], 71), 0)
    keys = draw_keys(jax.random.fold_in(seeds[9], 71), 0)
    values = centred(seeds[6], (TOKENS, AC), 1.0, 6.0, ((0, 32), (1, 8)))
    lengths = uneven(seeds[7], GENOMES, TOKENS, MOST, 2).astype(jnp.int32)
    w_out = noise_with(seeds[8], (AC, D), AC ** -0.5, 0.125, ((0, 8),), (0, 1, 8, 2.0))
    return {"residual": residual, "streams": streams, "short_filter": short_filter, "medium_filter": medium_filter, "queries": queries, "keys": keys, "values": values, "lengths": lengths, "w_out": w_out}


def genome_of(lengths, positions):
    ends = jnp.cumsum(lengths).astype(jnp.int32)
    return jnp.sum((ends[None, :] <= positions[:, None]).astype(jnp.int32), axis=1).astype(jnp.int32)


def featurize(streams, short_filter, genome):
    row_count = streams.shape[0]
    tap_count = short_filter.shape[0]
    data = streams.astype(jnp.float32)
    padded = jnp.pad(data, ((tap_count - 1, 0), (0, 0), (0, 0)))
    genome_pad = jnp.concatenate([jnp.full((tap_count - 1,), -1, jnp.int32), genome])
    featured = jnp.zeros(data.shape, jnp.float32)
    for lag_index in range(tap_count):
        start_row = tap_count - 1 - lag_index
        same_genome = genome_pad[start_row:start_row + row_count] == genome
        term = padded[start_row:start_row + row_count] * short_filter[lag_index].astype(jnp.float32)[None]
        featured = featured + jnp.where(same_genome[:, None, None], term, 0.0)
    return featured.astype(jnp.bfloat16)


def medium_conv(product, medium_filter, genome):
    row_count = product.shape[0]
    block_size = 128
    group_count = medium_filter.shape[1]
    group_width = product.shape[1] // group_count
    block_count = row_count // block_size
    block_index = jnp.arange(block_size)
    lag_table = (block_index[:, None] - block_index[None, :]) % block_size
    toeplitz = jnp.transpose(medium_filter.astype(jnp.float32)[lag_table], (2, 0, 1))
    causal = block_index[:, None] >= block_index[None, :]
    lower = jnp.where(causal[None], toeplitz, 0.0)
    upper = jnp.where(causal[None], 0.0, toeplitz)
    data = lax.optimization_barrier(product).astype(jnp.float32)
    current = data.reshape(block_count, block_size, group_count, group_width)
    earlier = jnp.concatenate([jnp.zeros((1, block_size, group_count, group_width), jnp.float32), current[:-1]], axis=0)
    genome_now = genome.reshape(block_count, block_size)
    genome_before = jnp.concatenate([jnp.full((1, block_size), -1, jnp.int32), genome_now[:-1]], axis=0)

    def one_block(operands):
        here, before, genome_here, genome_prev = operands
        same_now = genome_here[:, None] == genome_here[None, :]
        same_prev = genome_here[:, None] == genome_prev[None, :]
        near_part = jnp.einsum('gts,sgc->tgc', lower * same_now[None], here, precision=lax.Precision.HIGHEST)
        far_part = jnp.einsum('gts,sgc->tgc', upper * same_prev[None], before, precision=lax.Precision.HIGHEST)
        return near_part + far_part

    medium = lax.map(one_block, (current, earlier, genome_now, genome_before))
    return medium.reshape(row_count, group_count * group_width)


def attend(queries, keys, values, genome):
    row_count = queries.shape[0]
    block_size = 128
    block_count = row_count // block_size
    score_scale = float(HD) ** -0.5
    key_heads = keys.astype(jnp.float32).reshape(row_count, HEADS, HD)
    value_heads = values.astype(jnp.float32).reshape(row_count, HEADS, HD)
    positions = jnp.arange(row_count, dtype=jnp.int32)
    query_blocks = queries.astype(jnp.float32).reshape(block_count, block_size, HEADS, HD)
    position_blocks = positions.reshape(block_count, block_size)
    genome_blocks = genome.reshape(block_count, block_size)

    def one_block(operands):
        query_block, query_pos, query_genome = operands
        scores = jnp.einsum('qhd,khd->hqk', query_block, key_heads, precision=lax.Precision.HIGHEST) * score_scale
        allowed = (positions[None, :] <= query_pos[:, None]) & (genome[None, :] == query_genome[:, None])
        scores = jnp.where(allowed[None], scores, -1e30)
        row_max = jnp.max(scores, axis=2, keepdims=True)
        exps = jnp.where(allowed[None], jnp.exp(scores - row_max), 0.0)
        denominator = jnp.sum(exps, axis=2)
        rounded = lax.optimization_barrier(exps.astype(jnp.bfloat16)).astype(jnp.float32)
        summed = jnp.einsum('hqk,khd->qhd', rounded, value_heads, precision=lax.Precision.HIGHEST)
        result = summed / jnp.transpose(denominator)[:, :, None]
        return result.astype(jnp.bfloat16).reshape(block_size, HEADS * HD)

    return lax.map(one_block, (query_blocks, position_blocks, genome_blocks)).reshape(row_count, HEADS * HD)


def reference(residual, streams, short_filter, medium_filter, queries, keys, values, lengths, w_out):
    genome = genome_of(lengths, jnp.arange(streams.shape[0], dtype=jnp.int32))
    featured = featurize(streams, short_filter, genome)
    featured_wide = lax.optimization_barrier(featured).astype(jnp.float32)
    product = (featured_wide[:, 1] * featured_wide[:, 2]).astype(jnp.bfloat16)
    medium = medium_conv(product, medium_filter, genome)
    hyena_mix = (featured_wide[:, 0] * medium).astype(jnp.bfloat16)
    attended = attend(queries, keys, values, genome)
    projected = jnp.dot(attended, w_out, preferred_element_type=jnp.float32)
    mixed = (residual.astype(jnp.float32) + projected).astype(jnp.bfloat16)
    return hyena_mix, attended, mixed
```

```python
import functools
import math

import jax
import jax.numpy as jnp
from jax import lax
from jax.experimental import pallas as pl
from jax.experimental.pallas import tpu as pltpu
from jax.sharding import PartitionSpec as P

HD = 128
ROWS = 256
GENOMES = 8
SHORT = 7
WIDE = 512
COLS = 1024
START = -1.0e30
NEVER = -2.0e30
LOG2 = math.log2(math.e) / math.sqrt(HD)
MESH = pl.DeviceIdType.MESH


def iota(shape, axis):
    return lax.broadcasted_iota(jnp.int32, shape, axis)


def kernel(
    lengths, residual, streams, short, medium, queries, keys, values, w_out,
    hyena, attended, mixed,
    qb, kb, vb, vt, gq, gk, mst, lst, acc, oth, ost, ob, att, wb, snd, rcv, res, mix,
    sb, f0, prod, hyo, lo_sem,
    a_send, a_recv, g_send, g_recv, h_send, h_recv, z_send, z_recv, r_send, r_recv,
    o_send, o_recv, w_send, w_recv, p_send, p_recv, n_send, n_recv,
):
    c, t = lax.axis_index("ctx"), lax.axis_index("tp")
    z, x, y = c // 16, lax.rem(c // 4, 4), lax.rem(c, 4)
    zh, p = t // 2, lax.rem(t, 2)
    a, b = x + (y - x) * p, y + (x - y) * p
    sa, sb_ = 4 - 3 * p, 1 + 3 * p

    def ring(v, d):
        return lax.rem(v + d, 4)

    def dev(a1, b1):
        return (16 * z + a1 * sa + b1 * sb_, t)

    def tile(a1, b1):
        return a1 * sa + b1 * sb_

    left, right = dev(a, ring(b, 3)), dev(a, ring(b, 1))
    across = (lax.rem(c + 16, 32), t)
    sibling = (c, t + 1 - 2 * p)
    up, down = (c, lax.rem(t + 2, 8)), (c, lax.rem(t + 6, 8))
    after, before = (lax.rem(c + 1, 32), t), (lax.rem(c + 31, 32), t)

    def remote(src, dst, send, recv, to):
        return pltpu.make_async_remote_copy(
            src_ref=src, dst_ref=dst, send_sem=send, recv_sem=recv, device_id=to, device_id_type=MESH
        )

    def head(ref, h):
        return ref.at[:, pl.ds(pl.multiple_of(h * HD, HD), HD)]

    me = tile(a, b)
    own = [
        pltpu.make_async_copy(head(keys, a), kb.at[me], lo_sem.at[0]),
        pltpu.make_async_copy(head(values, a), vb.at[me], lo_sem.at[1]),
        pltpu.make_async_copy(head(queries, a), qb.at[a], lo_sem.at[2]),
    ]
    for copy in own:
        copy.start()
    streams_in = pltpu.make_async_copy(streams, sb.at[:, pl.ds(16, ROWS)], lo_sem.at[3])
    streams_in.start()
    residual_in = pltpu.make_async_copy(residual, res, lo_sem.at[4])

    def block_cols(j, parity):
        return w_out.at[:, pl.ds(pl.multiple_of((2 * j + parity) * COLS, COLS), COLS)]

    weights_in = [
        pltpu.make_async_copy(block_cols(j, p), wb.at[p, j], lo_sem.at[5 + j]) for j in range(4)
    ]

    barrier = pltpu.get_barrier_semaphore()
    partners = [dev(ring(a, d), b) for d in (1, 2, 3)] + [
        left, right, across, sibling, up, down, after, before,
    ]
    for to in partners:
        pl.semaphore_signal(barrier, inc=1, device_id=to, device_id_type=MESH)
    pl.semaphore_wait(barrier, len(partners))

    def spread(d, i):
        to_a = ring(a, d)
        src = (keys, values, queries)[i]
        dst = (kb.at[me], vb.at[me], qb.at[a])[i]
        return remote(head(src, to_a), dst, a_send.at[d, i], a_recv.at[d, i], dev(to_a, b))

    def spread_in(d, i):
        from_a = ring(a, 4 - d)
        dst = (kb.at[tile(from_a, b)], vb.at[tile(from_a, b)], qb.at[from_a])[i]
        return remote(dst, dst, a_send.at[d, i], a_recv.at[d, i], dev(from_a, b))

    for d in (1, 3, 2):
        for i in range(3):
            spread(d, i).start()
    halo = remote(
        streams.at[:, pl.ds(ROWS - 16, 16)], sb.at[:, pl.ds(0, 16)], h_send.at[0], h_recv.at[0], after
    )
    halo.start()
    swap = [
        remote(block_cols(j, 1 - p), wb.at[p, j], w_send.at[j], w_recv.at[j], sibling) for j in range(4)
    ]
    for copy in weights_in + swap + [residual_in]:
        copy.start()

    def gather(d, i, way):
        j = tile(ring(a, 4 - d), b)
        ref = (kb, vb)[i].at[j]
        to = right if way == 0 else left
        return remote(ref, ref, g_send.at[0, d, i, way], g_recv.at[0, d, i, way], to)

    def gather_in(d, i, way):
        j = tile(ring(a, 4 - d), ring(b, 3 if way == 0 else 1))
        ref = (kb, vb)[i].at[j]
        return remote(ref, ref, g_send.at[0, d, i, way], g_recv.at[0, d, i, way], left)

    def onward(d, i):
        j = tile(ring(a, 4 - d), ring(b, 3 if i == 0 else 1))
        ref = (kb, vb)[i].at[j]
        to = right if i == 0 else left
        return remote(ref, ref, g_send.at[1, d, i, 0], g_recv.at[1, d, i, 0], to)

    def onward_in(d, i):
        ref = (kb, vb)[i].at[tile(ring(a, 4 - d), ring(b, 2))]
        return remote(ref, ref, g_send.at[1, d, i, 0], g_recv.at[1, d, i, 0], left)

    def visit(d):
        i = ring(a, 4 - d)
        return remote(qb.at[i], qb.at[4 + i], z_send.at[d], z_recv.at[d], across)

    def pass_on(d):
        for i in range(2):
            for way in range(2):
                gather(d, i, way).start()

    for copy in own:
        copy.wait()
    pass_on(0)

    @pl.when(z == 1)
    def _():
        visit(0).start()
        qb[4:8] = jnp.zeros((4, ROWS, HD), jnp.bfloat16)

    starts, ends, total = [], [], jnp.int32(0)
    for j in range(GENOMES):
        starts.append(total)
        total = total + lengths[j]
        ends.append(total)
    lane = iota((1, HD), 1)
    first_of, end_of = jnp.zeros((1, HD), jnp.int32), jnp.zeros((1, HD), jnp.int32)
    for j in range(GENOMES):
        first_of = jnp.where(lane == j, starts[j], first_of)
        end_of = jnp.where(lane == j, ends[j], end_of)

    def inside(position):
        spot = position + iota((ROWS, HD), 0)
        return (spot >= first_of) & (spot < end_of)

    @pl.loop(0, 16)
    def _(j):
        gk[j] = jnp.where(inside((16 * z + j) * ROWS), 0.0, NEVER).astype(jnp.bfloat16)

    @pl.loop(0, 8)
    def _(i):
        j = tile(lax.rem(i, 4), b) + 16 * jnp.where(i >= 4, 1, z)
        gq[i] = jnp.where(inside(j * ROWS), 1.0, 0.0).astype(jnp.bfloat16)

    mst[...] = jnp.full(mst.shape, START, jnp.float32)
    lst[...] = jnp.zeros(lst.shape, jnp.float32)
    acc[...] = jnp.zeros(acc.shape, jnp.float32)

    for d in (1, 3, 2):
        spread_in(d, 0).wait_recv()
        spread_in(d, 1).wait_recv()
        pass_on(d)
        spread_in(d, 2).wait_recv()

        @pl.when(z == 1)
        def _():
            visit(d).start()

    streams_in.wait()
    halo.wait_recv()
    base = c * ROWS
    spot = base + iota((ROWS, HD), 0)
    first = jnp.zeros((ROWS, HD), jnp.int32)
    for j in range(1, GENOMES):
        first = jnp.where(spot >= starts[j], starts[j], first)
    depth = spot - first

    @pl.loop(0, 4)
    def _(n):
        lanes = pl.ds(pl.multiple_of(n * HD, HD), HD)
        made = []
        for j in range(3):
            data = sb[j, :, lanes].astype(jnp.float32)
            taps = short[j, :, lanes].astype(jnp.float32)
            total = data[16:] * taps[0:1]
            for lag in range(1, SHORT):
                moved = pltpu.roll(data, lag, 0)[16:]
                total = total + jnp.where(depth >= lag, moved * taps[lag : lag + 1], 0.0)
            made.append(total.astype(jnp.bfloat16))
        f0[n] = made[0]
        prod[n, pl.ds(128, ROWS)] = (
            made[1].astype(jnp.float32) * made[2].astype(jnp.float32)
        ).astype(jnp.bfloat16)

    tail = remote(
        prod.at[:, pl.ds(ROWS, 128)], prod.at[:, pl.ds(0, 128)], h_send.at[1], h_recv.at[1], after
    )
    tail.start()

    @pl.when(z == 0)
    def _():
        for d in range(4):
            i = ring(a, 4 - d)
            remote(qb.at[4 + i], qb.at[4 + i], z_send.at[d], z_recv.at[d], across).wait_recv()

    def attend(ks, ss, offs):
        scores = []
        for i in range(4):
            q = ss[i] if ss[i] is None else jnp.minimum(ss[i], 7)
            wide_k = jnp.concatenate([kb[ks[i]], gk[ks[i]]], axis=1)
            wide_q = jnp.concatenate([qb[q], gq[q]], axis=1)
            s = lax.dot_general(
                wide_k, wide_q, (((1,), (1,)), ((), ())), preferred_element_type=jnp.float32
            )
            if offs is not None:
                ahead = iota((ROWS, ROWS), 0) - iota((ROWS, ROWS), 1)
                s = jnp.where(ahead <= offs[i], s, NEVER)
            scores.append(s)
        old = [mst[ss[i]] for i in range(4)]
        new = [
            jnp.maximum(old[i], jnp.max(scores[i], axis=0, keepdims=True)) for i in range(4)
        ]
        exps = [jnp.exp2(scores[i] * LOG2 - new[i][0:1] * LOG2) for i in range(4)]
        fade = [jnp.exp2((old[i] - new[i]) * LOG2) for i in range(4)]
        sums = [
            lst[ss[i]] * fade[i] + jnp.sum(exps[i].reshape(ROWS // 8, 8, ROWS), axis=0)
            for i in range(4)
        ]
        outs = [
            acc[ss[i]] * fade[i][0:1]
            + jnp.dot(vt[ks[i]], exps[i].astype(jnp.bfloat16), preferred_element_type=jnp.float32)
            for i in range(4)
        ]
        for i in range(4):
            mst[ss[i]] = new[i]
            lst[ss[i]] = sums[i]
            acc[ss[i]] = outs[i]

    slots = [tile(i, b) for i in range(4)]

    def turn(j):
        vt[j] = vb[j].astype(jnp.float32).T.astype(jnp.bfloat16)

    @pl.loop(0, 5)
    def _(n):
        d = jnp.minimum(n, 3)
        j = tile(ring(a, 4 - d), b)

        @pl.when(n < 4)
        def _():
            turn(j)

        ks = [jnp.where(n < 4, j, slots[i]) for i in range(4)]
        ss = [i + 4 * jnp.where((n == 4) | (j > slots[i]), 1, 0) for i in range(4)]
        offs = [
            jnp.where(ss[i] >= 4, ROWS, (slots[i] - ks[i]) * ROWS) for i in range(4)
        ]
        attend(ks, ss, offs)

    @pl.loop(0, 13)
    def _(n):
        near = n < 8
        d = jnp.where(near, n // 2, jnp.minimum(n, 11) - 8)
        side = jnp.where(near, 3 - 2 * lax.rem(n, 2), 2)
        j = tile(ring(a, 4 - d), ring(b, side))

        @pl.when(near & (side == 3))
        def _():
            gather_in(d, 0, 0).wait_recv()
            onward(d, 0).start()
            gather_in(d, 1, 0).wait_recv()

        @pl.when(near & (side == 1))
        def _():
            gather_in(d, 1, 1).wait_recv()
            onward(d, 1).start()
            gather_in(d, 0, 1).wait_recv()

        @pl.when((n >= 8) & (n < 12))
        def _():
            onward_in(d, 0).wait_recv()
            onward_in(d, 1).wait_recv()

        @pl.when(n < 12)
        def _():
            turn(j)

        last = n == 12
        ks = [jnp.where(last, jnp.maximum(slots[i] - 1, 0), j) for i in range(4)]
        ss = [
            jnp.where(
                last & (slots[i] == 0), 8, i + 4 * jnp.where(last | (j > slots[i]), 1, 0)
            )
            for i in range(4)
        ]
        attend(ks, ss, None)

    def give(i):
        return [
            remote(oth.at[0, i], oth.at[1, i], r_send.at[0, i], r_recv.at[0, i], across),
            remote(ost.at[0, i], ost.at[1, i], r_send.at[1, i], r_recv.at[1, i], across),
        ]

    def close(i):
        total = jnp.sum(lst[i], axis=0, keepdims=True)
        return total, acc[i] / jnp.maximum(total, 1.0e-30)

    @pl.when(z == 0)
    def _():
        for i in range(4):
            total, out = close(4 + i)
            oth[0, i] = out.astype(jnp.bfloat16)
            ost[0, i, 0] = mst[4 + i]
            ost[0, i, 1] = jnp.broadcast_to(total, (8, ROWS))
            for copy in give(i):
                copy.start()

    def home(d):
        to_a = ring(a, d)
        return remote(ob.at[to_a], att.at[p, a], o_send.at[d], o_recv.at[d], dev(to_a, b))

    def home_in(d):
        ref = att.at[p, ring(a, 4 - d)]
        return remote(ref, ref, o_send.at[d], o_recv.at[d], dev(ring(a, 4 - d), b))

    for d in (1, 2, 3, 0):
        i = ring(a, d)
        total, out = close(i)
        ob[i] = out.T.astype(jnp.bfloat16)

        @pl.when(z == 1)
        def _():
            for copy in give(i):
                copy.wait_recv()
            m_other, l_other = ost[1, i, 0, 0:1], ost[1, i, 1, 0:1]
            m_own = mst[i, 0:1]
            top = jnp.maximum(m_own, m_other)
            w_own = jnp.exp2((m_own - top) * LOG2) * total
            w_other = jnp.exp2((m_other - top) * LOG2) * l_other
            both = (out * w_own + oth[1, i].astype(jnp.float32) * w_other) / (w_own + w_other)
            ob[i] = both.T.astype(jnp.bfloat16)

        if d > 0:
            home(d).start()
        else:
            att[p, a] = ob[i]
    for d in (1, 2, 3):
        home_in(d).wait_recv()
    cross = remote(att.at[p], att.at[p], n_send.at[0], n_recv.at[0], sibling)
    cross.start()
    attended_out = [
        pltpu.make_async_copy(att.at[p, i], head(attended, i), lo_sem.at[9 + i]) for i in range(4)
    ]
    for copy in attended_out:
        copy.start()
    rcv[:, 0] = jnp.zeros((2, 2, 128, WIDE), jnp.bfloat16)
    for copy in weights_in:
        copy.wait()
    for j in range(4):
        remote(wb.at[1 - p, j], wb.at[1 - p, j], w_send.at[j], w_recv.at[j], sibling).wait_recv()
    residual_in.wait()
    tail.wait_recv()
    cross_in = remote(att.at[1 - p], att.at[1 - p], n_send.at[0], n_recv.at[0], sibling)
    cross_in.wait_recv()

    def sum_step(step, half, way):
        return remote(
            snd.at[way, step, half], rcv.at[way, step + 1, half],
            p_send.at[way, step, half], p_recv.at[way, step + 1, half], (up, down)[way],
        )

    def sum_in(step, half, way):
        ref = rcv.at[way, step, half]
        return remote(ref, ref, p_send.at[way, 0, half], p_recv.at[way, step, half], (down, up)[way])

    flip = jnp.where(
        lax.rem(iota((128, 128), 0) + iota((128, 128), 1), 128) == 0, 1.0, 0.0
    ).astype(jnp.bfloat16)
    taps_back = jnp.dot(medium[...], flip, preferred_element_type=jnp.float32)
    hyo_taps = taps_back

    def genome_at(position):
        genome = jnp.zeros(position.shape, jnp.int32)
        for j in range(GENOMES):
            genome = genome + jnp.where(position >= ends[j], 1, 0)
        return genome

    mst[0:4, :, 0:128] = hyo_taps.reshape(4, 8, 128)

    def convolve(n):
        lt, blk = n // 2, lax.rem(n, 2)
        here = base + blk * 128
        rows, cols = iota((128, 128), 0), iota((128, 128), 1)
        genome_now = genome_at(here + rows)
        genome_src = genome_at(here + cols)
        earlier = here - 128 + cols
        genome_prev = genome_at(earlier)
        near = (genome_now == genome_src) & (rows >= cols)
        far = (genome_now == genome_prev) & (rows < cols) & (earlier >= 0)
        data = prod[lt, pl.ds(pl.multiple_of(blk * 128, 128), 256)]
        band = iota((128, 128), 1) // 16
        out = jnp.zeros((128, 128), jnp.float32)
        for g in range(8):
            taps = jnp.broadcast_to(mst[lt, g : g + 1, 0:128], (128, 128))
            around = pltpu.roll(taps, 0, 1, stride=1, stride_axis=0)
            weights = jnp.concatenate(
                [jnp.where(far, around, 0.0), jnp.where(near, around, 0.0)], axis=1
            ).astype(jnp.bfloat16)
            term = jnp.dot(weights, data, preferred_element_type=jnp.float32)
            out = jnp.where(band == g, term, out)
        place = pl.ds(pl.multiple_of(blk * 128, 128), 128)
        hyo[lt, place] = (f0[lt, place].astype(jnp.float32) * out).astype(jnp.bfloat16)

    @pl.loop(0, 8)
    def _(n):
        step, half = n // 2, lax.rem(n, 2)
        place = pl.ds(pl.multiple_of(half * 128, 128), 128)
        for way in range(2):
            j = ring(zh, 3 - step if way == 0 else 1 + step)
            part = jnp.zeros((128, WIDE), jnp.float32)
            for k in range(2):
                rows = jnp.concatenate([att[k, i, place] for i in range(4)], axis=1)
                part = part + jnp.dot(
                    rows, wb[k, j, :, way * WIDE : (way + 1) * WIDE],
                    preferred_element_type=jnp.float32,
                )

            @pl.when(step > 0)
            def _():
                sum_in(step, half, way).wait_recv()

            part = part + rcv[way, step, half].astype(jnp.float32)

            @pl.when(step < 3)
            def _():
                snd[way, step, half] = part.astype(jnp.bfloat16)
                sum_step(step, half, way).start()

            @pl.when(step == 3)
            def _():
                lanes = slice(way * WIDE, (way + 1) * WIDE)
                mix[place, lanes] = (
                    res[place, lanes].astype(jnp.float32) + part
                ).astype(jnp.bfloat16)

        convolve(n)

    outs = [
        pltpu.make_async_copy(hyo.at[i], head(hyena, i), lo_sem.at[i]) for i in range(4)
    ] + [pltpu.make_async_copy(mix, mixed, lo_sem.at[4])]
    for copy in outs:
        copy.start()

    for d in (1, 2, 3):
        for i in range(3):
            spread(d, i).wait_send()
        home(d).wait_send()
    halo.wait_send()
    tail.wait_send()
    cross.wait_send()
    for copy in swap:
        copy.wait_send()
    for d in range(4):
        for i in range(2):
            for way in range(2):
                gather(d, i, way).wait_send()
            onward(d, i).wait_send()

    @pl.when(z == 1)
    def _():
        for d in range(4):
            visit(d).wait_send()

    @pl.when(z == 0)
    def _():
        for i in range(4):
            for copy in give(i):
                copy.wait_send()

    for way in range(2):
        for step in range(3):
            for half in range(2):
                sum_step(step, half, way).wait_send()
    for copy in outs + attended_out:
        copy.wait()


def body(residual, streams, short_filter, medium_filter, queries, keys, values, lengths, w_out):
    bf16, f32 = jnp.bfloat16, jnp.float32
    anywhere = pl.BlockSpec(memory_space=pl.ANY)
    vmem = pl.BlockSpec(memory_space=pltpu.VMEM)
    dma = pltpu.SemaphoreType.DMA
    scratch = [
        pltpu.VMEM((8, ROWS, HD), bf16),
        pltpu.VMEM((16, ROWS, HD), bf16),
        pltpu.VMEM((16, ROWS, HD), bf16),
        pltpu.VMEM((16, HD, ROWS), bf16),
        pltpu.VMEM((8, ROWS, HD), bf16),
        pltpu.VMEM((16, ROWS, HD), bf16),
        pltpu.VMEM((9, 8, ROWS), f32),
        pltpu.VMEM((9, 8, ROWS), f32),
        pltpu.VMEM((9, HD, ROWS), f32),
        pltpu.VMEM((2, 4, HD, ROWS), bf16),
        pltpu.VMEM((2, 4, 2, 8, ROWS), f32),
        pltpu.VMEM((4, ROWS, HD), bf16),
        pltpu.VMEM((2, 4, ROWS, HD), bf16),
        pltpu.VMEM((2, 4, 512, COLS), bf16),
        pltpu.VMEM((2, 3, 2, 128, WIDE), bf16),
        pltpu.VMEM((2, 4, 2, 128, WIDE), bf16),
        pltpu.VMEM((ROWS, COLS), bf16),
        pltpu.VMEM((ROWS, COLS), bf16),
        pltpu.VMEM((3, ROWS + 16, 512), bf16),
        pltpu.VMEM((4, ROWS, HD), bf16),
        pltpu.VMEM((4, ROWS + 128, HD), bf16),
        pltpu.VMEM((4, ROWS, HD), bf16),
        dma((13,)),
        dma((4, 3)), dma((4, 3)),
        dma((2, 4, 2, 2)), dma((2, 4, 2, 2)),
        dma((2,)), dma((2,)),
        dma((4,)), dma((4,)),
        dma((2, 4)), dma((2, 4)),
        dma((4,)), dma((4,)),
        dma((4,)), dma((4,)),
        dma((2, 3, 2)), dma((2, 4, 2)),
        dma((1,)), dma((1,)),
    ]
    return pl.pallas_call(
        kernel,
        out_shape=(
            jax.ShapeDtypeStruct((ROWS, 512), bf16),
            jax.ShapeDtypeStruct((ROWS, 512), bf16),
            jax.ShapeDtypeStruct((ROWS, COLS), bf16),
        ),
        in_specs=[
            pl.BlockSpec(memory_space=pltpu.SMEM), anywhere, anywhere, vmem, vmem,
            anywhere, anywhere, anywhere, anywhere,
        ],
        out_specs=(anywhere, anywhere, anywhere),
        scratch_shapes=scratch,
        compiler_params=pltpu.CompilerParams(
            collective_id=0, has_side_effects=True, vmem_limit_bytes=56 * 1024 * 1024
        ),
        cost_estimate=pl.CostEstimate(
            flops=7_000_000_000, bytes_accessed=16_000_000, transcendentals=5_000_000
        ),
        name="mixer",
    )(
        lengths, residual, jnp.transpose(streams, (1, 0, 2)), jnp.transpose(short_filter, (1, 0, 2)),
        medium_filter.T, queries, keys, values, w_out,
    )


def solution(mesh):
    in_specs = (
        P("ctx", "tp"),
        P("ctx", None, "tp"),
        P(None, None, "tp"),
        P(None, "tp"),
        P("ctx", "tp"),
        P("ctx", "tp"),
        P("ctx", "tp"),
        P(),
        P("tp", None),
    )
    out_specs = (P("ctx", "tp"), P("ctx", "tp"), P("ctx", "tp"))
    return jax.shard_map(body, mesh=mesh, in_specs=in_specs, out_specs=out_specs, check_vma=False)
```

```python
import functools
import math

import jax
import jax.numpy as jnp
from jax import lax
from jax.experimental import pallas as pl
from jax.experimental.pallas import tpu as pltpu
from jax.sharding import PartitionSpec as P

HD = 128
ROWS = 256
GENOMES = 8
SHORT = 7
WIDE = 512
COLS = 1024
START = -1.0e30
NEVER = -2.0e30
LOG2 = math.log2(math.e) / math.sqrt(HD)
MESH = pl.DeviceIdType.MESH
FAR = (0, 1)
EARLY = False
CONTROL = {"ls": {1: 8, 3: 9}, "lo": {1: 15, 3: 16}, "ps": {}}


def iota(shape, axis):
    return lax.broadcasted_iota(jnp.int32, shape, axis)


def kernel(
    lengths_in, residual, streams, short_in, medium_in, queries, keys, values, w_out,
    hyena, attended, mixed,
    lengths, short, medium, plain, tq, tv, qt, even, odd, kb, vt, gk, mst, lst, acc, oth, ost, ob, att, wb, sums, res, mix,
    taps_ref, sb, f0, prod, hyo, lo_sem,
    a_send, a_recv, g_send, g_recv, h_send, h_recv, z_send, z_recv, r_send, r_recv,
    o_send, o_recv, w_send, w_recv, s_send, s_recv, l_send, l_recv, m_send, m_recv,
    p_send, p_recv, n_send, n_recv,
):
    c, t = lax.axis_index("ctx"), lax.axis_index("tp")
    z, x, y = c // 16, lax.rem(c // 4, 4), lax.rem(c, 4)
    zh, p = t // 2, lax.rem(t, 2)
    a, b = x + (y - x) * p, y + (x - y) * p
    sa, sb_ = 4 - 3 * p, 1 + 3 * p

    def ring(v, d):
        return lax.rem(v + d, 4)

    def dev(a1, b1):
        return (16 * z + a1 * sa + b1 * sb_, t)

    def tile(a1, b1):
        return a1 * sa + b1 * sb_

    left, right = dev(a, ring(b, 3)), dev(a, ring(b, 1))
    across = (lax.rem(c + 16, 32), t)
    sibling = (c, t + 1 - 2 * p)
    after, before = (lax.rem(c + 1, 32), t), (lax.rem(c + 31, 32), t)

    def remote(src, dst, send, recv, to):
        return pltpu.make_async_remote_copy(
            src_ref=src, dst_ref=dst, send_sem=send, recv_sem=recv, device_id=to, device_id_type=MESH
        )

    def head(ref, h):
        return ref.at[:, pl.ds(pl.multiple_of(h * HD, HD), HD)]

    me = tile(a, b)
    both_in = [
        pltpu.make_async_copy(queries, plain.at[0], lo_sem.at[2]),
        pltpu.make_async_copy(values, plain.at[1], lo_sem.at[1]),
    ]
    small_in = [
        pltpu.make_async_copy(lengths_in, lengths, lo_sem.at[13]),
        pltpu.make_async_copy(short_in, short, lo_sem.at[14]),
        pltpu.make_async_copy(medium_in, medium, lo_sem.at[15]),
    ]
    own = pltpu.make_async_copy(head(keys, a), kb.at[me], lo_sem.at[0])
    for copy in both_in + small_in + [own]:
        copy.start()
    streams_in = pltpu.make_async_copy(streams, sb.at[:, pl.ds(16, ROWS)], lo_sem.at[3])
    streams_in.start()
    residual_in = pltpu.make_async_copy(residual, res, lo_sem.at[4])

    def block_cols(j, rows):
        return w_out.at[rows, :, pl.ds(pl.multiple_of(j * COLS, COLS), COLS)]

    every = pl.ds(0, 16)
    weights_in = pltpu.make_async_copy(block_cols(t, every), wb.at[0, p], lo_sem.at[5])
    over_z = [
        (c, lax.rem(2 * zh + 2 * d, 8) + core) for d in (1, 2, 3) for core in range(2)
    ]

    barrier = pltpu.get_barrier_semaphore()
    partners = [dev(ring(a, d), b) for d in (1, 2, 3)] + over_z + [
        left, right, across, sibling, after, before,
    ]
    for to in partners:
        pl.semaphore_signal(barrier, inc=1, device_id=to, device_id_type=MESH)
    for i, copy in enumerate(both_in):
        copy.wait()
        for h in range(4):
            turned = plain[i, :, h * HD : (h + 1) * HD].astype(jnp.float32).T
            (tq, tv)[i][h] = turned.astype(jnp.bfloat16)
    top = pl.ds(0, HD)
    qt[a, 0:HD] = tq[a]
    vt[me] = tv[a]
    pl.semaphore_wait(barrier, len(partners))

    def spread(d, i):
        to_a = ring(a, d)
        src = (head(keys, to_a), tv.at[to_a], tq.at[to_a])[i]
        dst = (kb.at[me], vt.at[me], qt.at[a, top])[i]
        return remote(src, dst, a_send.at[d, i], a_recv.at[d, i], dev(to_a, b))

    def spread_in(d, i):
        from_a = ring(a, 4 - d)
        dst = (kb.at[tile(from_a, b)], vt.at[tile(from_a, b)], qt.at[from_a, top])[i]
        return remote(dst, dst, a_send.at[d, i], a_recv.at[d, i], dev(from_a, b))

    for i in (2, 0, 1):
        for d in (1, 3, 2):
            spread(d, i).start()
    halo = remote(
        streams.at[:, pl.ds(ROWS - 16, 16)], sb.at[:, pl.ds(0, 16)], h_send.at[0], h_recv.at[0], after
    )
    halo.start()
    swap = remote(
        block_cols(t + 1 - 2 * p, every), wb.at[0, p], w_send.at[0], w_recv.at[0], sibling
    )

    def shard(d, core):
        spot = y * 4 + x + (x * 4 + y - y * 4 - x) * core
        to = lax.rem(2 * zh + 2 * d, 8) + core
        return remote(
            block_cols(to, spot), wb.at[4 - d, p, spot],
            s_send.at[d, core], s_recv.at[d, p], (c, to),
        )

    def shard_in(d, core):
        ref = wb.at[4 - d, core, 4 * b + a]
        return remote(ref, ref, s_send.at[d, core], s_recv.at[d, core], sibling)

    for d in (3, 1):
        for core in range(2):
            shard(d, core).start()

    def shards_start():
        for core in range(2):
            shard(2, core).start()
        for copy in (weights_in, swap, residual_in):
            copy.start()

    prev_a, next_a = dev(ring(a, 3), b), dev(ring(a, 1), b)
    pair = pl.ds(0, 2)

    def line(k, op):
        e, here = k, 4 * b
        ref = (
            wb.at[e, pair, here + a], wb.at[e, pair, here + a],
            wb.at[e, 0, here + ring(a, 3)], wb.at[e, 1, here + ring(a, 1)],
        )[op]
        to = next_a if op % 2 == 0 else prev_a
        return remote(ref, ref, l_send.at[k, op], l_recv.at[k, op], to)

    def line_in(k, op):
        e, here = k, 4 * b
        ref = (
            wb.at[e, pair, here + ring(a, 3)], wb.at[e, pair, here + ring(a, 1)],
            wb.at[e, 0, here + ring(a, 2)], wb.at[e, 1, here + ring(a, 2)],
        )[op]
        return remote(ref, ref, l_send.at[k, op], l_recv.at[k, op], next_a)

    def block(k, core, d):
        return wb.at[k, core, pl.ds(4 * ring(b, d), 4)]

    def plane(k, op):
        ref = block(k, (0, 1, 0, 1, 0, 1)[op], (0, 0, 0, 0, 3, 1)[op])
        to = right if op in (0, 1, 4) else left
        return remote(ref, ref, m_send.at[k, op], m_recv.at[k, op], to)

    def plane_in(k, op):
        ref = block(k, (0, 1, 0, 1, 0, 1)[op], (3, 3, 1, 1, 2, 2)[op])
        return remote(ref, ref, m_send.at[k, op], m_recv.at[k, op], left)

    def line_start(k):
        for core in range(2):
            shard_in(4 - k, core).wait_recv()
        line(k, 0).start()
        line(k, 1).start()

    def line_onward(k):
        line_in(k, 0).wait_recv()
        line(k, 2).start()
        line_in(k, 1).wait_recv()
        line(k, 3).start()

    def plane_start(k):
        line_in(k, 2).wait_recv()
        line_in(k, 3).wait_recv()
        for op in (0, 3, 1, 2):
            plane(k, op).start()

    def plane_onward(k):
        plane_in(k, 0).wait_recv()
        plane(k, 4).start()
        plane_in(k, 3).wait_recv()
        plane(k, 5).start()

    def plane_wait(k):
        for op in (1, 2, 4, 5):
            plane_in(k, op).wait_recv()

    def gather(d, i, way):
        j = tile(ring(a, 4 - d), b)
        ref = (kb, vt)[i].at[j]
        to = right if way == 0 else left
        return remote(ref, ref, g_send.at[0, d, i, way], g_recv.at[0, d, i, way], to)

    def gather_in(d, i, way):
        j = tile(ring(a, 4 - d), ring(b, 3 if way == 0 else 1))
        ref = (kb, vt)[i].at[j]
        return remote(ref, ref, g_send.at[0, d, i, way], g_recv.at[0, d, i, way], left)

    def onward(d, i):
        j = tile(ring(a, 4 - d), ring(b, 3 if FAR[i] == 0 else 1))
        ref = (kb, vt)[i].at[j]
        to = right if FAR[i] == 0 else left
        return remote(ref, ref, g_send.at[1, d, i, 0], g_recv.at[1, d, i, 0], to)

    def onward_in(d, i):
        ref = (kb, vt)[i].at[tile(ring(a, 4 - d), ring(b, 2))]
        return remote(ref, ref, g_send.at[1, d, i, 0], g_recv.at[1, d, i, 0], left)

    def visit(d):
        i = ring(a, 4 - d)
        return remote(qt.at[i, top], qt.at[4 + i, top], z_send.at[d], z_recv.at[d], across)

    def pass_on(d):
        for i in range(2):
            for way in range(2):
                gather(d, i, way).start()

    own.wait()
    pass_on(0)

    @pl.when(z == 1)
    def _():
        visit(0).start()

    for copy in small_in:
        copy.wait()
    starts, ends, total = [], [], jnp.int32(0)
    for j in range(GENOMES):
        starts.append(total)
        total = total + lengths[j]
        ends.append(total)
    def bounds(index):
        low, high = jnp.zeros(index.shape, jnp.int32), jnp.zeros(index.shape, jnp.int32)
        for j in range(GENOMES):
            low = jnp.where(index == j, starts[j], low)
            high = jnp.where(index == j, ends[j], high)
        return low, high

    def inside(position, axis, limits):
        spot = position + iota((ROWS, HD) if axis == 0 else (HD, ROWS), axis)
        return (spot >= limits[0]) & (spot < limits[1])

    by_lane, by_row = bounds(iota((1, HD), 1)), bounds(iota((HD, 1), 0))

    @pl.loop(0, 16)
    def _(j):
        gk[j] = jnp.where(inside((16 * z + j) * ROWS, 0, by_lane), 0.0, NEVER).astype(jnp.bfloat16)

    @pl.loop(0, 8)
    def _(i):
        j = tile(lax.rem(i, 4), b) + 16 * jnp.where(i >= 4, 1, z)
        qt[i, HD:] = jnp.where(inside(j * ROWS, 1, by_row), 1.0, 0.0).astype(jnp.bfloat16)

    mst[...] = jnp.full(mst.shape, START, jnp.float32)
    lst[...] = jnp.zeros(lst.shape, jnp.float32)
    acc[...] = jnp.zeros(acc.shape, jnp.float32)

    for d in (1, 3, 2):
        spread_in(d, 2).wait_recv()

        @pl.when(z == 1)
        def _():
            visit(d).start()

    shards_start()
    for d in (1, 3, 2):
        spread_in(d, 0).wait_recv()
        spread_in(d, 1).wait_recv()
        pass_on(d)

    slots = [tile(i, b) for i in range(4)]

    def fetch(n):
        near, far = (n >= 4) & (n < 12), (n >= 12) & (n < 16)
        d = jnp.where(near, n // 2 - 2, jnp.where(far, n - 12, 0))
        side = jnp.where(near, 3 - 2 * lax.rem(n, 2), jnp.where(far, 2, 0))
        j = step_tile(n)

        @pl.when((z == 0) & (n > 0) & (n < 5))
        def _():
            ref = qt.at[3 + n, top]
            remote(
                ref, ref, z_send.at[0], z_recv.at[ring(a, 5 - n)], across
            ).wait_recv()

        @pl.when(near & (side == 3))
        def _():
            for i in range(2):
                gather_in(d, i, 0).wait_recv()
                if FAR[i] == 0:
                    onward(d, i).start()

        @pl.when(near & (side == 1))
        def _():
            for i in range(2):
                gather_in(d, i, 1).wait_recv()
                if FAR[i] == 1:
                    onward(d, i).start()

        @pl.when(far)
        def _():
            onward_in(d, 0).wait_recv()
            onward_in(d, 1).wait_recv()

        return plan(n, j)

    def plan(n, j):
        same, prior = n == 16, n == 17
        ks = [
            jnp.where(same, slots[i], jnp.where(prior, jnp.maximum(slots[i] - 1, 0), j))
            for i in range(4)
        ]
        ss = [
            jnp.where(
                prior & (slots[i] == 0), 8, i + 4 * jnp.where(same | prior | (j > slots[i]), 1, 0)
            )
            for i in range(4)
        ]
        return j, ks, ss

    def score(k, s, buf, i):
        q = jnp.minimum(s, 7)
        wide_k = jnp.concatenate([kb[k], gk[k]], axis=1)
        buf[i] = jnp.dot(wide_k, qt[q], preferred_element_type=jnp.float32)

    def weigh(k, s, buf, i):
        scores, old = buf[i], mst[s]
        new = jnp.maximum(old, jnp.max(scores, axis=0, keepdims=True))
        exps = jnp.exp2(scores * LOG2 - new[0:1] * LOG2)
        fade = jnp.exp2((old - new) * LOG2)
        mst[s] = new
        lst[s] = lst[s] * fade + jnp.sum(exps.reshape(ROWS // 8, 8, ROWS), axis=0)
        acc[s] = acc[s] * fade[0:1] + jnp.dot(
            vt[k], exps.astype(jnp.bfloat16), preferred_element_type=jnp.float32
        )

    def causal(n, buf):
        @pl.when(n < 4)
        def _():
            ahead = iota((ROWS, ROWS), 0) <= iota((ROWS, ROWS), 1)
            buf[n] = jnp.where(ahead, buf[n], NEVER)

    def step(n, buf, following):
        _, ks_next, ss_next = fetch(jnp.minimum(n + 1, 17))
        for act, times in CONTROL.items():
            act = {"ls": line_start, "lo": line_onward, "ps": plane_start}[act]
            for k in times:

                @pl.when(n == times[k])
                def _():
                    act(k)

        _, ks, ss = plan(n, step_tile(n))
        for i in range(4):
            score(ks_next[i], ss_next[i], following, i)
            weigh(ks[i], ss[i], buf, i)
        causal(n + 1, following)

    def step_tile(n):
        near, far = (n >= 4) & (n < 12), (n >= 12) & (n < 16)
        d = jnp.where(near, n // 2 - 2, jnp.where(far, n - 12, 0))
        side = jnp.where(near, 3 - 2 * lax.rem(n, 2), jnp.where(far, 2, 0))
        own_line = jnp.where(n < 4, n, 3)
        return tile(jnp.where(near | far, ring(a, 4 - d), own_line), ring(b, side))

    @pl.when(z == 1)
    def _():
        qt[4:8, 0:HD] = jnp.zeros((4, HD, ROWS), jnp.bfloat16)

    _, first_ks, first_ss = plan(jnp.int32(0), tile(0, b))
    for i in range(4):
        score(first_ks[i], first_ss[i], even, i)
    causal(jnp.int32(0), even)

    @pl.loop(0, 9)
    def _(n):
        step(2 * n, even, odd)
        step(2 * n + 1, odd, even)

    def give(i):
        return [
            remote(oth.at[0, i], oth.at[1, i], r_send.at[0, i], r_recv.at[0, i], across),
            remote(ost.at[0, i], ost.at[1, i], r_send.at[1, i], r_recv.at[1, i], across),
        ]

    def close(i):
        total = jnp.sum(lst[i], axis=0, keepdims=True)
        return total, acc[i] * (1.0 / jnp.maximum(total, 1.0e-30))

    base = c * ROWS
    tail = remote(
        prod.at[:, pl.ds(ROWS, 128)], prod.at[:, pl.ds(0, 128)], h_send.at[1], h_recv.at[1], after
    )

    def featurize():
        streams_in.wait()
        halo.wait_recv()
        spot = base + iota((ROWS, HD), 0)
        first = jnp.zeros((ROWS, HD), jnp.int32)
        for j in range(1, GENOMES):
            first = jnp.where(spot >= starts[j], starts[j], first)
        depth = spot - first

        @pl.loop(0, 4)
        def _(n):
            lanes = pl.ds(pl.multiple_of(n * HD, HD), HD)
            made = []
            for j in range(3):
                data = sb[j, :, lanes].astype(jnp.float32)
                taps = short[j, :, lanes].astype(jnp.float32)
                total = data[16:] * taps[0:1]
                for lag in range(1, SHORT):
                    moved = pltpu.roll(data, lag, 0)[16:]
                    total = total + jnp.where(depth >= lag, moved * taps[lag : lag + 1], 0.0)
                made.append(total.astype(jnp.bfloat16))
            f0[n] = made[0]
            prod[n, pl.ds(128, ROWS)] = (
                made[1].astype(jnp.float32) * made[2].astype(jnp.float32)
            ).astype(jnp.bfloat16)
        tail.start()

    def chores():
        line_start(2)
        for k in (1, 3):
            if k not in CONTROL["lo"]:
                line_onward(k)
        for k in (1, 3):
            if k not in CONTROL["ps"]:
                plane_start(k)
        featurize()
        line_onward(2)
        if EARLY:
            plane_start(2)
        plane_onward(1)

    def home(d):
        to_a = ring(a, d)
        return remote(ob.at[to_a], att.at[0, p, a], o_send.at[d], o_recv.at[d], dev(to_a, b))

    def home_in(d):
        ref = att.at[0, p, ring(a, 4 - d)]
        return remote(ref, ref, o_send.at[d], o_recv.at[d], dev(ring(a, 4 - d), b))

    if "ls" not in CONTROL:
        for k in (1, 3):
            line_start(k)

    @pl.when(z == 1)
    def _():
        chores()

    for d in (1, 2, 3, 0):
        i = ring(a, d)
        total, out = close(i)
        ob[i] = out.T.astype(jnp.bfloat16)

        @pl.when(z == 1)
        def _():
            for copy in give(i):
                copy.wait_recv()
            m_other, l_other = ost[1, i, 0, 0:1], ost[1, i, 1, 0:1]
            m_own = mst[i, 0:1]
            top = jnp.maximum(m_own, m_other)
            w_own = jnp.exp2((m_own - top) * LOG2) * total
            w_other = jnp.exp2((m_other - top) * LOG2) * l_other
            share = 1.0 / (w_own + w_other)
            both = out * (w_own * share) + oth[1, i].astype(jnp.float32) * (w_other * share)
            ob[i] = both.T.astype(jnp.bfloat16)

        if d > 0:
            home(d).start()
        else:
            att[0, p, a] = ob[i]

    up, down = (c, lax.rem(t + 2, 8)), (c, lax.rem(t + 6, 8))
    halves = (pl.ds(0, 2), pl.ds(2, 2))

    def climb(op):
        half = (0, 1, 0, 1, 0, 1)[op]
        src = (0, 0, 0, 0, 3, 1)[op]
        dst = (3, 3, 1, 1, 2, 2)[op]
        to = up if op in (0, 1, 4) else down
        return remote(
            att.at[src, p, halves[half]], att.at[dst, p, halves[half]],
            p_send.at[op], p_recv.at[op], to,
        )

    def climb_in(op):
        ref = att.at[(3, 3, 1, 1, 2, 2)[op], p, halves[op % 2]]
        return remote(ref, ref, p_send.at[op], p_recv.at[op], up)

    def cross(op):
        ref = att.at[0, p] if op == 6 else att.at[(3, 3, 1, 1, 2, 2)[op], p, halves[op % 2]]
        return remote(ref, ref, n_send.at[op], n_recv.at[op], sibling)

    def cross_in(op):
        q = 1 - p
        ref = att.at[0, q] if op == 6 else att.at[(3, 3, 1, 1, 2, 2)[op], q, halves[op % 2]]
        return remote(ref, ref, n_send.at[op], n_recv.at[op], sibling)

    def multiply(e):
        rows = jnp.concatenate([att[e, core, i] for core in range(2) for i in range(4)], axis=1)

        @pl.loop(0, 2)
        def _(n):
            lanes = pl.ds(pl.multiple_of(n * 512, 512), 512)
            w = wb[e, :, :, :, lanes].reshape(1024, 512)
            sums[:, lanes] += jnp.dot(rows, w, preferred_element_type=jnp.float32)

    flip = jnp.where(
        lax.rem(iota((128, 128), 0) + iota((128, 128), 1), 128) == 0, 1.0, 0.0
    ).astype(jnp.bfloat16)
    taps_back = jnp.dot(medium[...], flip, preferred_element_type=jnp.float32)
    hyo_taps = taps_back

    def genome_at(position):
        genome = jnp.zeros(position.shape, jnp.int32)
        for j in range(GENOMES):
            genome = genome + jnp.where(position >= ends[j], 1, 0)
        return genome

    taps_ref[...] = hyo_taps.reshape(4, 8, 128)

    def convolve(n):
        lt, blk = n // 2, lax.rem(n, 2)
        here = base + blk * 128
        rows, cols = iota((128, 128), 0), iota((128, 128), 1)
        genome_now = genome_at(here + rows)
        genome_src = genome_at(here + cols)
        earlier = here - 128 + cols
        genome_prev = genome_at(earlier)
        near = (genome_now == genome_src) & (rows >= cols)
        far = (genome_now == genome_prev) & (rows < cols) & (earlier >= 0)
        data = prod[lt, pl.ds(pl.multiple_of(blk * 128, 128), 256)]
        band = iota((128, 128), 1) // 16
        out = jnp.zeros((128, 128), jnp.float32)
        for g in range(8):
            taps = jnp.broadcast_to(taps_ref[lt, g : g + 1], (128, 128))
            around = pltpu.roll(taps, 0, 1, stride=1, stride_axis=0)
            weights = jnp.concatenate(
                [jnp.where(far, around, 0.0), jnp.where(near, around, 0.0)], axis=1
            ).astype(jnp.bfloat16)
            term = jnp.dot(weights, data, preferred_element_type=jnp.float32)
            out = jnp.where(band == g, term, out)
        place = pl.ds(pl.multiple_of(blk * 128, 128), 128)
        hyo[lt, place] = (f0[lt, place].astype(jnp.float32) * out).astype(jnp.bfloat16)

    @pl.when(z == 0)
    def _():
        for i in range(4):
            total, out = close(4 + i)
            oth[0, i] = out.astype(jnp.bfloat16)
            ost[0, i, 0] = mst[4 + i]
            ost[0, i, 1] = jnp.broadcast_to(total, (8, ROWS))
            for copy in give(i):
                copy.start()

    @pl.when(z == 0)
    def _():
        chores()

    for d in (1, 2, 3):
        home_in(d).wait_recv()
    for op in (0, 3, 1, 2):
        climb(op).start()
    cross(6).start()
    attended_out = [
        pltpu.make_async_copy(att.at[0, p, i], head(attended, i), lo_sem.at[6 + i]) for i in range(4)
    ]
    for copy in attended_out:
        copy.start()
    residual_in.wait()
    sums[...] = res[...].astype(jnp.float32)
    if not EARLY:
        plane_start(2)
    tail.wait_recv()

    @pl.loop(0, 4)
    def _(n):
        convolve(n)

    plane_onward(3)
    climb_in(0).wait_recv()
    climb(4).start()
    cross(0).start()
    climb_in(3).wait_recv()
    climb(5).start()
    cross(3).start()

    plane_onward(2)

    @pl.loop(4, 8)
    def _(n):
        convolve(n)

    hyena_out = [
        pltpu.make_async_copy(hyo.at[i], head(hyena, i), lo_sem.at[i]) for i in range(4)
    ]
    for copy in hyena_out:
        copy.start()
    weights_in.wait()
    cross_in(6).wait_recv()
    remote(wb.at[0, 1 - p], wb.at[0, 1 - p], w_send.at[0], w_recv.at[0], sibling).wait_recv()
    multiply(0)
    for op in (1, 2):
        climb_in(op).wait_recv()
        cross(op).start()
    for d in (1, 2, 3):
        for i in range(3):
            spread(d, i).wait_send()
        home(d).wait_send()
        for core in range(2):
            shard(d, core).wait_send()
        for op in range(4):
            line(d, op).wait_send()
    halo.wait_send()
    tail.wait_send()
    swap.wait_send()
    for d in range(4):
        for i in range(2):
            for way in range(2):
                gather(d, i, way).wait_send()
            onward(d, i).wait_send()

    @pl.when(z == 1)
    def _():
        for d in range(4):
            visit(d).wait_send()

    @pl.when(z == 0)
    def _():
        for i in range(4):
            for copy in give(i):
                copy.wait_send()

    for copy in hyena_out + attended_out:
        copy.wait()
    for e, ops in ((1, (2, 3)), (3, (0, 1)), (2, (4, 5))):
        if e == 2:
            for op in ops:
                climb_in(op).wait_recv()
                cross(op).start()
        plane_wait(e)
        for op in ops:
            cross_in(op).wait_recv()
        if e != 2:
            multiply(e)
    rows = jnp.concatenate([att[2, core, i] for core in range(2) for i in range(4)], axis=1)
    mixed_out = []
    for n in range(2):
        lanes = slice(n * 512, (n + 1) * 512)
        w = wb[2, :, :, :, lanes].reshape(1024, 512)
        mix[:, lanes] = (
            sums[:, lanes] + jnp.dot(rows, w, preferred_element_type=jnp.float32)
        ).astype(jnp.bfloat16)
        mixed_out.append(pltpu.make_async_copy(mix.at[:, lanes], mixed.at[:, lanes], lo_sem.at[4 + n]))
        mixed_out[n].start()

    for d in (1, 2, 3):
        for op in range(6):
            plane(d, op).wait_send()
    for op in range(6):
        climb(op).wait_send()
    for op in range(7):
        cross(op).wait_send()
    for copy in mixed_out:
        copy.wait()


def hand_out(a_in, b_in, c_in, a_out, b_out, c_out, a_mid, b_mid, c_mid, sem):
    parts = [
        (src.at[rows], mid.at[rows], dst.at[rows], sem.at[n, i])
        for n, (src, mid, dst) in enumerate(
            ((a_in, a_mid, a_out), (b_in, b_mid, b_out), (c_in, c_mid, c_out))
        )
        for i, rows in enumerate((pl.ds(0, 128), pl.ds(128, 128)))
    ]
    first = [pltpu.make_async_copy(src, mid, s.at[0]) for src, mid, _, s in parts]
    second = [pltpu.make_async_copy(mid, dst, s.at[1]) for _, mid, dst, s in parts]
    for copy in first:
        copy.start()
    for one, two in zip(first, second):
        one.wait()
        two.start()
    for copy in second:
        copy.wait()


def body(residual, streams, short_filter, medium_filter, queries, keys, values, lengths, w_out):
    bf16, f32 = jnp.bfloat16, jnp.float32
    anywhere = pl.BlockSpec(memory_space=pl.ANY)
    dma = pltpu.SemaphoreType.DMA
    scratch = [
        pltpu.SMEM((GENOMES,), jnp.int32),
        pltpu.VMEM((3, SHORT, 512), bf16),
        pltpu.VMEM((32, 128), bf16),
        pltpu.VMEM((2, ROWS, 512), bf16),
        pltpu.VMEM((4, HD, ROWS), bf16),
        pltpu.VMEM((4, HD, ROWS), bf16),
        pltpu.VMEM((8, 2 * HD, ROWS), bf16),
        pltpu.VMEM((4, ROWS, ROWS), f32),
        pltpu.VMEM((4, ROWS, ROWS), f32),
        pltpu.VMEM((16, ROWS, HD), bf16),
        pltpu.VMEM((16, HD, ROWS), bf16),
        pltpu.VMEM((16, ROWS, HD), bf16),
        pltpu.VMEM((9, 8, ROWS), f32),
        pltpu.VMEM((9, 8, ROWS), f32),
        pltpu.VMEM((9, HD, ROWS), f32),
        pltpu.VMEM((2, 4, HD, ROWS), bf16),
        pltpu.VMEM((2, 4, 2, 8, ROWS), f32),
        pltpu.VMEM((4, ROWS, HD), bf16),
        pltpu.VMEM((4, 2, 4, ROWS, HD), bf16),
        pltpu.VMEM((4, 2, 16, 32, COLS), bf16),
        pltpu.VMEM((ROWS, COLS), f32),
        pltpu.VMEM((ROWS, COLS), bf16),
        pltpu.VMEM((ROWS, COLS), bf16),
        pltpu.VMEM((4, 8, 128), f32),
        pltpu.VMEM((3, ROWS + 16, 512), bf16),
        pltpu.VMEM((4, ROWS, HD), bf16),
        pltpu.VMEM((4, ROWS + 128, HD), bf16),
        pltpu.VMEM((4, ROWS, HD), bf16),
        dma((16,)),
        dma((4, 3)), dma((4, 3)),
        dma((2, 4, 2, 2)), dma((2, 4, 2, 2)),
        dma((2,)), dma((2,)),
        dma((4,)), dma((4,)),
        dma((2, 4)), dma((2, 4)),
        dma((4,)), dma((4,)),
        dma((1,)), dma((1,)),
        dma((4, 2)), dma((4, 2)),
        dma((4, 4)), dma((4, 4)),
        dma((4, 6)), dma((4, 6)),
        dma((6,)), dma((6,)),
        dma((7,)), dma((7,)),
    ]
    made = pl.pallas_call(
        kernel,
        out_shape=(
            jax.ShapeDtypeStruct((ROWS, 512), bf16),
            jax.ShapeDtypeStruct((ROWS, 512), bf16),
            jax.ShapeDtypeStruct((ROWS, COLS), bf16),
        ),
        in_specs=[anywhere] * 9,
        out_specs=(anywhere, anywhere, anywhere),
        scratch_shapes=scratch,
        compiler_params=pltpu.CompilerParams(
            collective_id=0, has_side_effects=True, vmem_limit_bytes=56 * 1024 * 1024
        ),
        cost_estimate=pl.CostEstimate(
            flops=7_000_000_000, bytes_accessed=16_000_000, transcendentals=5_000_000
        ),
        name="mixer",
    )(
        lengths, residual, jnp.transpose(streams, (1, 0, 2)), jnp.transpose(short_filter, (1, 0, 2)),
        medium_filter.T, queries, keys, values, w_out.reshape(16, 32, 8192),
    )
    return pl.pallas_call(
        hand_out,
        out_shape=tuple(jax.ShapeDtypeStruct(v.shape, v.dtype) for v in made),
        in_specs=[anywhere] * 3,
        out_specs=(anywhere,) * 3,
        scratch_shapes=[pltpu.VMEM(v.shape, v.dtype) for v in made] + [dma((3, 2, 2))],
        name="hand_out",
    )(*made)


def solution(mesh):
    in_specs = (
        P("ctx", "tp"),
        P("ctx", None, "tp"),
        P(None, None, "tp"),
        P(None, "tp"),
        P("ctx", "tp"),
        P("ctx", "tp"),
        P("ctx", "tp"),
        P(),
        P("tp", None),
    )
    out_specs = (P("ctx", "tp"), P("ctx", "tp"), P("ctx", "tp"))
    return jax.shard_map(body, mesh=mesh, in_specs=in_specs, out_specs=out_specs, check_vma=False)
```

```python
import functools
import math

import jax
import jax.numpy as jnp
from jax import lax
from jax.experimental import pallas as pl
from jax.experimental.pallas import tpu as pltpu
from jax.sharding import PartitionSpec as P

HD = 128
ROWS = 256
GENOMES = 8
SHORT = 7
WIDE = 512
COLS = 1024
START = -1.0e30
NEVER = -2.0e30
LOG2 = math.log2(math.e) / math.sqrt(HD)
MESH = pl.DeviceIdType.MESH
FAR = (0, 1)
LINES = ((8, 1, True), (9, 3, True), (15, 1, False), (16, 3, False))


def iota(shape, axis):
    return lax.broadcasted_iota(jnp.int32, shape, axis)


def kernel(
    lengths_in, residual, streams, short_in, medium_in, queries, keys, values, w_out,
    hyena, attended, mixed,
    lengths, short, medium, plain, tq, tv, qt, even, odd, kb, vt, gk, mst, lst, acc, oth, ost, ob, att, wb, sums, res, mix,
    taps_ref, sb, f0, prod, hyo, lo_sem,
    a_send, a_recv, g_send, g_recv, h_send, h_recv, z_send, z_recv, r_send, r_recv,
    o_send, o_recv, w_send, w_recv, s_send, s_recv, l_send, l_recv, m_send, m_recv,
    p_send, p_recv, n_send, n_recv,
):
    c, t = lax.axis_index("ctx"), lax.axis_index("tp")
    z, x, y = c // 16, lax.rem(c // 4, 4), lax.rem(c, 4)
    zh, p = t // 2, lax.rem(t, 2)
    a, b = x + (y - x) * p, y + (x - y) * p
    sa, sb_ = 4 - 3 * p, 1 + 3 * p

    def ring(v, d):
        return lax.rem(v + d, 4)

    def dev(a1, b1):
        return (16 * z + a1 * sa + b1 * sb_, t)

    def tile(a1, b1):
        return a1 * sa + b1 * sb_

    left, right = dev(a, ring(b, 3)), dev(a, ring(b, 1))
    across = (lax.rem(c + 16, 32), t)
    sibling = (c, t + 1 - 2 * p)
    after, before = (lax.rem(c + 1, 32), t), (lax.rem(c + 31, 32), t)

    def remote(src, dst, send, recv, to):
        return pltpu.make_async_remote_copy(
            src_ref=src, dst_ref=dst, send_sem=send, recv_sem=recv, device_id=to, device_id_type=MESH
        )

    def head(ref, h):
        return ref.at[:, pl.ds(pl.multiple_of(h * HD, HD), HD)]

    me = tile(a, b)
    both_in = [
        pltpu.make_async_copy(queries, plain.at[0], lo_sem.at[2]),
        pltpu.make_async_copy(values, plain.at[1], lo_sem.at[1]),
    ]
    small_in = [
        pltpu.make_async_copy(lengths_in, lengths, lo_sem.at[13]),
        pltpu.make_async_copy(short_in, short, lo_sem.at[14]),
        pltpu.make_async_copy(medium_in, medium, lo_sem.at[15]),
    ]
    own = pltpu.make_async_copy(head(keys, a), kb.at[me], lo_sem.at[0])
    for copy in both_in + small_in + [own]:
        copy.start()
    streams_in = pltpu.make_async_copy(streams, sb.at[:, pl.ds(16, ROWS)], lo_sem.at[3])
    streams_in.start()
    residual_in = pltpu.make_async_copy(residual, res, lo_sem.at[4])

    def block_cols(j, rows):
        return w_out.at[rows, :, pl.ds(pl.multiple_of(j * COLS, COLS), COLS)]

    every = pl.ds(0, 16)
    weights_in = pltpu.make_async_copy(block_cols(t, every), wb.at[0, p], lo_sem.at[5])
    over_z = [
        (c, lax.rem(2 * zh + 2 * d, 8) + core) for d in (1, 2, 3) for core in range(2)
    ]

    barrier = pltpu.get_barrier_semaphore()
    partners = [dev(ring(a, d), b) for d in (1, 2, 3)] + over_z + [
        left, right, across, sibling, after, before,
    ]
    for to in partners:
        pl.semaphore_signal(barrier, inc=1, device_id=to, device_id_type=MESH)
    for i, copy in enumerate(both_in):
        copy.wait()
        for h in range(4):
            turned = plain[i, :, h * HD : (h + 1) * HD].astype(jnp.float32).T
            (tq, tv)[i][h] = turned.astype(jnp.bfloat16)
    top = pl.ds(0, HD)
    qt[a, 0:HD] = tq[a]
    vt[me] = tv[a]
    pl.semaphore_wait(barrier, len(partners))

    def spread(d, i):
        to_a = ring(a, d)
        src = (head(keys, to_a), tv.at[to_a], tq.at[to_a])[i]
        dst = (kb.at[me], vt.at[me], qt.at[a, top])[i]
        return remote(src, dst, a_send.at[d - 1, i], a_recv.at[d - 1, i], dev(to_a, b))

    def spread_in(d, i):
        from_a = ring(a, 4 - d)
        dst = (kb.at[tile(from_a, b)], vt.at[tile(from_a, b)], qt.at[from_a, top])[i]
        return remote(dst, dst, a_send.at[d - 1, i], a_recv.at[d - 1, i], dev(from_a, b))

    for i in (2, 0, 1):
        for d in (1, 3, 2):
            spread(d, i).start()
    halo = remote(
        streams.at[:, pl.ds(ROWS - 16, 16)], sb.at[:, pl.ds(0, 16)], h_send.at[0], h_recv.at[0], after
    )
    halo.start()
    swap = remote(
        block_cols(t + 1 - 2 * p, every), wb.at[0, p], w_send.at[0], w_recv.at[0], sibling
    )

    def shard(d, core):
        spot = y * 4 + x + (x * 4 + y - y * 4 - x) * core
        to = lax.rem(2 * zh + 2 * d, 8) + core
        return remote(
            block_cols(to, spot), wb.at[4 - d, p, spot],
            s_send.at[d - 1, core], s_recv.at[d - 1, p], (c, to),
        )

    def shard_in(d, core):
        ref = wb.at[4 - d, core, 4 * b + a]
        return remote(ref, ref, s_send.at[d - 1, core], s_recv.at[d - 1, core], sibling)

    for d in (3, 1):
        for core in range(2):
            shard(d, core).start()

    def shards_start():
        for core in range(2):
            shard(2, core).start()
        for copy in (weights_in, swap, residual_in):
            copy.start()

    prev_a, next_a = dev(ring(a, 3), b), dev(ring(a, 1), b)
    pair = pl.ds(0, 2)

    def line(k, op):
        e, here = k, 4 * b
        ref = (
            wb.at[e, pair, here + a], wb.at[e, pair, here + a],
            wb.at[e, 0, here + ring(a, 3)], wb.at[e, 1, here + ring(a, 1)],
        )[op]
        to = next_a if op % 2 == 0 else prev_a
        return remote(ref, ref, l_send.at[k - 1, op], l_recv.at[k - 1, op], to)

    def line_in(k, op):
        e, here = k, 4 * b
        ref = (
            wb.at[e, pair, here + ring(a, 3)], wb.at[e, pair, here + ring(a, 1)],
            wb.at[e, 0, here + ring(a, 2)], wb.at[e, 1, here + ring(a, 2)],
        )[op]
        return remote(ref, ref, l_send.at[k - 1, op], l_recv.at[k - 1, op], next_a)

    def block(k, core, d):
        return wb.at[k, core, pl.ds(4 * ring(b, d), 4)]

    def plane(k, op):
        ref = block(k, (0, 1, 0, 1, 0, 1)[op], (0, 0, 0, 0, 3, 1)[op])
        to = right if op in (0, 1, 4) else left
        return remote(ref, ref, m_send.at[k - 1, op], m_recv.at[k - 1, op], to)

    def plane_in(k, op):
        ref = block(k, (0, 1, 0, 1, 0, 1)[op], (3, 3, 1, 1, 2, 2)[op])
        return remote(ref, ref, m_send.at[k - 1, op], m_recv.at[k - 1, op], left)

    def line_start(k):
        for core in range(2):
            shard_in(4 - k, core).wait_recv()
        line(k, 0).start()
        line(k, 1).start()

    def line_onward(k):
        line_in(k, 0).wait_recv()
        line(k, 2).start()
        line_in(k, 1).wait_recv()
        line(k, 3).start()

    def plane_start(k):
        line_in(k, 2).wait_recv()
        line_in(k, 3).wait_recv()
        for op in (0, 3, 1, 2):
            plane(k, op).start()

    def plane_onward(k):
        plane_in(k, 0).wait_recv()
        plane(k, 4).start()
        plane_in(k, 3).wait_recv()
        plane(k, 5).start()

    def plane_wait(k):
        for op in (1, 2, 4, 5):
            plane_in(k, op).wait_recv()

    def gather(d, i, way):
        j = tile(ring(a, 4 - d), b)
        ref = (kb, vt)[i].at[j]
        to = right if way == 0 else left
        return remote(ref, ref, g_send.at[d, 2 * i + way], g_recv.at[d, 2 * i + way], to)

    def gather_in(d, i, way):
        j = tile(ring(a, 4 - d), ring(b, 3 if way == 0 else 1))
        ref = (kb, vt)[i].at[j]
        return remote(ref, ref, g_send.at[d, 2 * i + way], g_recv.at[d, 2 * i + way], left)

    def onward(d, i):
        j = tile(ring(a, 4 - d), ring(b, 3 if FAR[i] == 0 else 1))
        ref = (kb, vt)[i].at[j]
        to = right if FAR[i] == 0 else left
        return remote(ref, ref, g_send.at[d, 4 + i], g_recv.at[d, 4 + i], to)

    def onward_in(d, i):
        ref = (kb, vt)[i].at[tile(ring(a, 4 - d), ring(b, 2))]
        return remote(ref, ref, g_send.at[d, 4 + i], g_recv.at[d, 4 + i], left)

    def visit(d):
        i = ring(a, 4 - d)
        return remote(qt.at[i, top], qt.at[4 + i, top], z_send.at[d], z_recv.at[d], across)

    def pass_on(d):
        for i in range(2):
            for way in range(2):
                gather(d, i, way).start()

    own.wait()
    pass_on(0)

    @pl.when(z == 1)
    def _():
        visit(0).start()

    for copy in small_in:
        copy.wait()
    starts, ends, total = [], [], jnp.int32(0)
    for j in range(GENOMES):
        starts.append(total)
        total = total + lengths[j]
        ends.append(total)
    def bounds(index):
        low, high = jnp.zeros(index.shape, jnp.int32), jnp.zeros(index.shape, jnp.int32)
        for j in range(GENOMES):
            low = jnp.where(index == j, starts[j], low)
            high = jnp.where(index == j, ends[j], high)
        return low, high

    def inside(position, axis, limits):
        spot = position + iota((ROWS, HD) if axis == 0 else (HD, ROWS), axis)
        return (spot >= limits[0]) & (spot < limits[1])

    by_lane, by_row = bounds(iota((1, HD), 1)), bounds(iota((HD, 1), 0))

    @pl.loop(0, 16)
    def _(j):
        gk[j] = jnp.where(inside((16 * z + j) * ROWS, 0, by_lane), 0.0, NEVER).astype(jnp.bfloat16)

    @pl.loop(0, 8)
    def _(i):
        j = tile(lax.rem(i, 4), b) + 16 * jnp.where(i >= 4, 1, z)
        qt[i, HD:] = jnp.where(inside(j * ROWS, 1, by_row), 1.0, 0.0).astype(jnp.bfloat16)

    mst[...] = jnp.full(mst.shape, START, jnp.float32)
    lst[...] = jnp.zeros(lst.shape, jnp.float32)
    acc[...] = jnp.zeros(acc.shape, jnp.float32)

    for d in (1, 3, 2):
        spread_in(d, 2).wait_recv()

        @pl.when(z == 1)
        def _():
            visit(d).start()

    shards_start()
    for d in (1, 3, 2):
        spread_in(d, 0).wait_recv()
        spread_in(d, 1).wait_recv()
        pass_on(d)

    slots = [tile(i, b) for i in range(4)]

    def fetch(n):
        near, far = (n >= 4) & (n < 12), (n >= 12) & (n < 16)
        d = jnp.where(near, n // 2 - 2, jnp.where(far, n - 12, 0))
        side = jnp.where(near, 3 - 2 * lax.rem(n, 2), jnp.where(far, 2, 0))
        j = step_tile(n)

        @pl.when((z == 0) & (n > 0) & (n < 5))
        def _():
            ref = qt.at[3 + n, top]
            remote(
                ref, ref, z_send.at[0], z_recv.at[ring(a, 5 - n)], across
            ).wait_recv()

        @pl.when(near & (side == 3))
        def _():
            for i in range(2):
                gather_in(d, i, 0).wait_recv()
                if FAR[i] == 0:
                    onward(d, i).start()

        @pl.when(near & (side == 1))
        def _():
            for i in range(2):
                gather_in(d, i, 1).wait_recv()
                if FAR[i] == 1:
                    onward(d, i).start()

        @pl.when(far)
        def _():
            onward_in(d, 0).wait_recv()
            onward_in(d, 1).wait_recv()

        return plan(n, j)

    def plan(n, j):
        same, prior = n == 16, n == 17
        ks = [
            jnp.where(same, slots[i], jnp.where(prior, jnp.maximum(slots[i] - 1, 0), j))
            for i in range(4)
        ]
        ss = [
            jnp.where(
                prior & (slots[i] == 0), 8, i + 4 * jnp.where(same | prior | (j > slots[i]), 1, 0)
            )
            for i in range(4)
        ]
        return j, ks, ss

    def score(k, s, buf, i):
        q = jnp.minimum(s, 7)
        wide_k = jnp.concatenate([kb[k], gk[k]], axis=1)
        buf[i] = jnp.dot(wide_k, qt[q], preferred_element_type=jnp.float32)

    def weigh(k, s, buf, i):
        scores, old = buf[i], mst[s]
        new = jnp.maximum(old, jnp.max(scores, axis=0, keepdims=True))
        exps = jnp.exp2(scores * LOG2 - new[0:1] * LOG2)
        fade = jnp.exp2((old - new) * LOG2)
        mst[s] = new
        lst[s] = lst[s] * fade + jnp.sum(exps.reshape(ROWS // 8, 8, ROWS), axis=0)
        acc[s] = acc[s] * fade[0:1] + jnp.dot(
            vt[k], exps.astype(jnp.bfloat16), preferred_element_type=jnp.float32
        )

    def causal(n, buf):
        @pl.when(n < 4)
        def _():
            ahead = iota((ROWS, ROWS), 0) <= iota((ROWS, ROWS), 1)
            buf[n] = jnp.where(ahead, buf[n], NEVER)

    def step(n, buf, following):
        _, ks_next, ss_next = fetch(jnp.minimum(n + 1, 17))
        for when, k, starts_line in LINES:

            @pl.when(n == when)
            def _():
                (line_start if starts_line else line_onward)(k)

        _, ks, ss = plan(n, step_tile(n))
        for i in range(4):
            score(ks_next[i], ss_next[i], following, i)
            weigh(ks[i], ss[i], buf, i)
        causal(n + 1, following)

    def step_tile(n):
        near, far = (n >= 4) & (n < 12), (n >= 12) & (n < 16)
        d = jnp.where(near, n // 2 - 2, jnp.where(far, n - 12, 0))
        side = jnp.where(near, 3 - 2 * lax.rem(n, 2), jnp.where(far, 2, 0))
        own_line = jnp.where(n < 4, n, 3)
        return tile(jnp.where(near | far, ring(a, 4 - d), own_line), ring(b, side))

    @pl.when(z == 1)
    def _():
        qt[4:8, 0:HD] = jnp.zeros((4, HD, ROWS), jnp.bfloat16)

    _, first_ks, first_ss = plan(jnp.int32(0), tile(0, b))
    for i in range(4):
        score(first_ks[i], first_ss[i], even, i)
    causal(jnp.int32(0), even)

    @pl.loop(0, 9)
    def _(n):
        step(2 * n, even, odd)
        step(2 * n + 1, odd, even)

    def give(i):
        return [
            remote(oth.at[0, i], oth.at[1, i], r_send.at[0, i], r_recv.at[0, i], across),
            remote(ost.at[0, i], ost.at[1, i], r_send.at[1, i], r_recv.at[1, i], across),
        ]

    def close(i):
        total = jnp.sum(lst[i], axis=0, keepdims=True)
        return total, acc[i] * (1.0 / jnp.maximum(total, 1.0e-30))

    base = c * ROWS
    tail = remote(
        prod.at[:, pl.ds(ROWS, 128)], prod.at[:, pl.ds(0, 128)], h_send.at[1], h_recv.at[1], after
    )

    def featurize():
        streams_in.wait()
        halo.wait_recv()
        spot = base + iota((ROWS, HD), 0)
        first = jnp.zeros((ROWS, HD), jnp.int32)
        for j in range(1, GENOMES):
            first = jnp.where(spot >= starts[j], starts[j], first)
        depth = spot - first

        @pl.loop(0, 4)
        def _(n):
            lanes = pl.ds(pl.multiple_of(n * HD, HD), HD)
            made = []
            for j in range(3):
                data = sb[j, :, lanes].astype(jnp.float32)
                taps = short[j, :, lanes].astype(jnp.float32)
                total = data[16:] * taps[0:1]
                for lag in range(1, SHORT):
                    moved = pltpu.roll(data, lag, 0)[16:]
                    total = total + jnp.where(depth >= lag, moved * taps[lag : lag + 1], 0.0)
                made.append(total.astype(jnp.bfloat16))
            f0[n] = made[0]
            prod[n, pl.ds(128, ROWS)] = (
                made[1].astype(jnp.float32) * made[2].astype(jnp.float32)
            ).astype(jnp.bfloat16)
        tail.start()

    def spread_weights():
        line_start(2)
        for k in (1, 3):
            plane_start(k)

    def chores():
        spread_weights()
        featurize()
        line_onward(2)

    def home(d):
        to_a = ring(a, d)
        return remote(ob.at[to_a], att.at[0, p, a], o_send.at[d - 1], o_recv.at[d - 1], dev(to_a, b))

    def home_in(d):
        ref = att.at[0, p, ring(a, 4 - d)]
        return remote(ref, ref, o_send.at[d - 1], o_recv.at[d - 1], dev(ring(a, 4 - d), b))

    @pl.when(z == 1)
    def _():
        chores()
        plane_onward(1)

    for d in (1, 2, 3, 0):
        i = ring(a, d)
        total, out = close(i)
        ob[i] = out.T.astype(jnp.bfloat16)

        @pl.when(z == 1)
        def _():
            for copy in give(i):
                copy.wait_recv()
            m_other, l_other = ost[1, i, 0, 0:1], ost[1, i, 1, 0:1]
            m_own = mst[i, 0:1]
            top = jnp.maximum(m_own, m_other)
            w_own = jnp.exp2((m_own - top) * LOG2) * total
            w_other = jnp.exp2((m_other - top) * LOG2) * l_other
            share = 1.0 / (w_own + w_other)
            both = out * (w_own * share) + oth[1, i].astype(jnp.float32) * (w_other * share)
            ob[i] = both.T.astype(jnp.bfloat16)

        if d > 0:
            home(d).start()
        else:
            att[0, p, a] = ob[i]

    up, down = (c, lax.rem(t + 2, 8)), (c, lax.rem(t + 6, 8))
    halves = (pl.ds(0, 2), pl.ds(2, 2))

    def climb(op):
        half = (0, 1, 0, 1, 0, 1)[op]
        src = (0, 0, 0, 0, 3, 1)[op]
        dst = (3, 3, 1, 1, 2, 2)[op]
        to = up if op in (0, 1, 4) else down
        return remote(
            att.at[src, p, halves[half]], att.at[dst, p, halves[half]],
            p_send.at[op], p_recv.at[op], to,
        )

    def climb_in(op):
        ref = att.at[(3, 3, 1, 1, 2, 2)[op], p, halves[op % 2]]
        return remote(ref, ref, p_send.at[op], p_recv.at[op], up)

    def cross(op):
        ref = att.at[0, p] if op == 6 else att.at[(3, 3, 1, 1, 2, 2)[op], p, halves[op % 2]]
        return remote(ref, ref, n_send.at[op], n_recv.at[op], sibling)

    def cross_in(op):
        q = 1 - p
        ref = att.at[0, q] if op == 6 else att.at[(3, 3, 1, 1, 2, 2)[op], q, halves[op % 2]]
        return remote(ref, ref, n_send.at[op], n_recv.at[op], sibling)

    def multiply(e):
        rows = jnp.concatenate([att[e, core, i] for core in range(2) for i in range(4)], axis=1)

        @pl.loop(0, 2)
        def _(n):
            lanes = pl.ds(pl.multiple_of(n * 512, 512), 512)
            w = wb[e, :, :, :, lanes].reshape(1024, 512)
            sums[:, lanes] += jnp.dot(rows, w, preferred_element_type=jnp.float32)

    flip = jnp.where(
        lax.rem(iota((128, 128), 0) + iota((128, 128), 1), 128) == 0, 1.0, 0.0
    ).astype(jnp.bfloat16)
    taps_back = jnp.dot(medium[...], flip, preferred_element_type=jnp.float32)
    hyo_taps = taps_back

    def genome_at(position):
        genome = jnp.zeros(position.shape, jnp.int32)
        for j in range(GENOMES):
            genome = genome + jnp.where(position >= ends[j], 1, 0)
        return genome

    taps_ref[...] = hyo_taps.reshape(4, 8, 128)

    def convolve(n):
        lt, blk = n // 2, lax.rem(n, 2)
        here = base + blk * 128
        rows, cols = iota((128, 128), 0), iota((128, 128), 1)
        genome_now = genome_at(here + rows)
        genome_src = genome_at(here + cols)
        earlier = here - 128 + cols
        genome_prev = genome_at(earlier)
        near = (genome_now == genome_src) & (rows >= cols)
        far = (genome_now == genome_prev) & (rows < cols) & (earlier >= 0)
        data = prod[lt, pl.ds(pl.multiple_of(blk * 128, 128), 256)]
        band = iota((128, 128), 1) // 16
        out = jnp.zeros((128, 128), jnp.float32)
        for g in range(8):
            taps = jnp.broadcast_to(taps_ref[lt, g : g + 1], (128, 128))
            around = pltpu.roll(taps, 0, 1, stride=1, stride_axis=0)
            weights = jnp.concatenate(
                [jnp.where(far, around, 0.0), jnp.where(near, around, 0.0)], axis=1
            ).astype(jnp.bfloat16)
            term = jnp.dot(weights, data, preferred_element_type=jnp.float32)
            out = jnp.where(band == g, term, out)
        place = pl.ds(pl.multiple_of(blk * 128, 128), 128)
        hyo[lt, place] = (f0[lt, place].astype(jnp.float32) * out).astype(jnp.bfloat16)

    @pl.when(z == 0)
    def _():
        for i in range(4):
            total, out = close(4 + i)
            oth[0, i] = out.astype(jnp.bfloat16)
            ost[0, i, 0] = mst[4 + i]
            ost[0, i, 1] = jnp.broadcast_to(total, (8, ROWS))
            for copy in give(i):
                copy.start()

    @pl.when(z == 0)
    def _():
        chores()

    for d in (1, 2, 3):
        home_in(d).wait_recv()
    for op in (0, 3, 1, 2):
        climb(op).start()
    cross(6).start()
    attended_out = [
        pltpu.make_async_copy(att.at[0, p, i], head(attended, i), lo_sem.at[6 + i]) for i in range(4)
    ]
    for copy in attended_out:
        copy.start()
    residual_in.wait()
    sums[...] = res[...].astype(jnp.float32)
    @pl.when(z == 0)
    def _():
        plane_onward(1)

    plane_start(2)
    tail.wait_recv()

    @pl.loop(0, 4)
    def _(n):
        convolve(n)

    plane_onward(3)
    climb_in(0).wait_recv()
    climb(4).start()
    cross(0).start()
    climb_in(3).wait_recv()
    climb(5).start()
    cross(3).start()

    plane_onward(2)

    @pl.loop(4, 8)
    def _(n):
        convolve(n)

    hyena_out = [
        pltpu.make_async_copy(hyo.at[i], head(hyena, i), lo_sem.at[i]) for i in range(4)
    ]
    for copy in hyena_out:
        copy.start()
    for op in (1, 2):
        climb_in(op).wait_recv()
        cross(op).start()
    weights_in.wait()
    cross_in(6).wait_recv()
    remote(wb.at[0, 1 - p], wb.at[0, 1 - p], w_send.at[0], w_recv.at[0], sibling).wait_recv()
    multiply(0)
    for d in (1, 2, 3):
        for i in range(3):
            spread(d, i).wait_send()
        home(d).wait_send()
        for core in range(2):
            shard(d, core).wait_send()
        for op in range(4):
            line(d, op).wait_send()
    halo.wait_send()
    tail.wait_send()
    swap.wait_send()
    for d in range(4):
        for i in range(2):
            for way in range(2):
                gather(d, i, way).wait_send()
            onward(d, i).wait_send()

    @pl.when(z == 1)
    def _():
        for d in range(4):
            visit(d).wait_send()

    @pl.when(z == 0)
    def _():
        for i in range(4):
            for copy in give(i):
                copy.wait_send()

    for copy in hyena_out + attended_out:
        copy.wait()
    for e, ops in ((1, (2, 3)), (3, (0, 1)), (2, (4, 5))):
        plane_wait(e)
        for op in ops:
            cross_in(op).wait_recv()
        if e == 1:
            for op in (4, 5):
                climb_in(op).wait_recv()
                cross(op).start()
        if e != 2:
            multiply(e)
    rows = jnp.concatenate([att[2, core, i] for core in range(2) for i in range(4)], axis=1)
    mixed_out = []
    for n in range(4):
        lanes = slice(n * 256, (n + 1) * 256)
        w = wb[2, :, :, :, lanes].reshape(1024, 256)
        mix[:, lanes] = (
            sums[:, lanes] + jnp.dot(rows, w, preferred_element_type=jnp.float32)
        ).astype(jnp.bfloat16)
        for m in range(2):
            place = (pl.ds(m * 128, 128), lanes)
            mixed_out.append(
                pltpu.make_async_copy(mix.at[place], mixed.at[place], lo_sem.at[(4, 5, 13, 14, 15, 10, 11, 12)[2 * n + m]])
            )
            mixed_out[-1].start()

    for d in (1, 2, 3):
        for op in range(6):
            plane(d, op).wait_send()
    for op in range(6):
        climb(op).wait_send()
    for op in range(7):
        cross(op).wait_send()
    for copy in mixed_out:
        copy.wait()


def hand_out(a_in, b_in, c_in, a_out, b_out, c_out, a_mid, b_mid, c_mid, sem):
    parts = [
        (src.at[rows], mid.at[rows], dst.at[rows], sem.at[n, i])
        for n, (src, mid, dst) in enumerate(
            ((a_in, a_mid, a_out), (b_in, b_mid, b_out), (c_in, c_mid, c_out))
        )
        for i, rows in enumerate((pl.ds(0, 128), pl.ds(128, 128)))
    ]
    first = [pltpu.make_async_copy(src, mid, s.at[0]) for src, mid, _, s in parts]
    second = [pltpu.make_async_copy(mid, dst, s.at[1]) for _, mid, dst, s in parts]
    for copy in first:
        copy.start()
    for one, two in zip(first, second):
        one.wait()
        two.start()
    for copy in second:
        copy.wait()


def body(residual, streams, short_filter, medium_filter, queries, keys, values, lengths, w_out):
    bf16, f32 = jnp.bfloat16, jnp.float32
    anywhere = pl.BlockSpec(memory_space=pl.ANY)
    dma = pltpu.SemaphoreType.DMA
    scratch = [
        pltpu.SMEM((GENOMES,), jnp.int32),
        pltpu.VMEM((3, SHORT, 512), bf16),
        pltpu.VMEM((32, 128), bf16),
        pltpu.VMEM((2, ROWS, 512), bf16),
        pltpu.VMEM((4, HD, ROWS), bf16),
        pltpu.VMEM((4, HD, ROWS), bf16),
        pltpu.VMEM((8, 2 * HD, ROWS), bf16),
        pltpu.VMEM((4, ROWS, ROWS), f32),
        pltpu.VMEM((4, ROWS, ROWS), f32),
        pltpu.VMEM((16, ROWS, HD), bf16),
        pltpu.VMEM((16, HD, ROWS), bf16),
        pltpu.VMEM((16, ROWS, HD), bf16),
        pltpu.VMEM((9, 8, ROWS), f32),
        pltpu.VMEM((9, 8, ROWS), f32),
        pltpu.VMEM((9, HD, ROWS), f32),
        pltpu.VMEM((2, 4, HD, ROWS), bf16),
        pltpu.VMEM((2, 4, 2, 8, ROWS), f32),
        pltpu.VMEM((4, ROWS, HD), bf16),
        pltpu.VMEM((4, 2, 4, ROWS, HD), bf16),
        pltpu.VMEM((4, 2, 16, 32, COLS), bf16),
        pltpu.VMEM((ROWS, COLS), f32),
        pltpu.VMEM((ROWS, COLS), bf16),
        pltpu.VMEM((ROWS, COLS), bf16),
        pltpu.VMEM((4, 8, 128), f32),
        pltpu.VMEM((3, ROWS + 16, 512), bf16),
        pltpu.VMEM((4, ROWS, HD), bf16),
        pltpu.VMEM((4, ROWS + 128, HD), bf16),
        pltpu.VMEM((4, ROWS, HD), bf16),
        dma((16,)),
        dma((3, 3)), dma((3, 3)),
        dma((4, 6)), dma((4, 6)),
        dma((2,)), dma((2,)),
        dma((4,)), dma((4,)),
        dma((2, 4)), dma((2, 4)),
        dma((4,)), dma((4,)),
        dma((1,)), dma((1,)),
        dma((3, 2)), dma((3, 2)),
        dma((3, 4)), dma((3, 4)),
        dma((3, 6)), dma((3, 6)),
        dma((6,)), dma((6,)),
        dma((7,)), dma((7,)),
    ]
    made = pl.pallas_call(
        kernel,
        out_shape=(
            jax.ShapeDtypeStruct((ROWS, 512), bf16),
            jax.ShapeDtypeStruct((ROWS, 512), bf16),
            jax.ShapeDtypeStruct((ROWS, COLS), bf16),
        ),
        in_specs=[anywhere] * 9,
        out_specs=(anywhere, anywhere, anywhere),
        scratch_shapes=scratch,
        compiler_params=pltpu.CompilerParams(
            collective_id=0, has_side_effects=True, vmem_limit_bytes=56 * 1024 * 1024
        ),
        cost_estimate=pl.CostEstimate(
            flops=7_000_000_000, bytes_accessed=16_000_000, transcendentals=5_000_000
        ),
        name="mixer",
    )(
        lengths, residual, jnp.transpose(streams, (1, 0, 2)), jnp.transpose(short_filter, (1, 0, 2)),
        medium_filter.T, queries, keys, values, w_out.reshape(16, 32, 8192),
    )
    return pl.pallas_call(
        hand_out,
        out_shape=tuple(jax.ShapeDtypeStruct(v.shape, v.dtype) for v in made),
        in_specs=[anywhere] * 3,
        out_specs=(anywhere,) * 3,
        scratch_shapes=[pltpu.VMEM(v.shape, v.dtype) for v in made] + [dma((3, 2, 2))],
        name="hand_out",
    )(*made)


def solution(mesh):
    in_specs = (
        P("ctx", "tp"),
        P("ctx", None, "tp"),
        P(None, None, "tp"),
        P(None, "tp"),
        P("ctx", "tp"),
        P("ctx", "tp"),
        P("ctx", "tp"),
        P(),
        P("tp", None),
    )
    out_specs = (P("ctx", "tp"), P("ctx", "tp"), P("ctx", "tp"))
    return jax.shard_map(body, mesh=mesh, in_specs=in_specs, out_specs=out_specs, check_vma=False)
```

```python
import functools
import math

import jax
import jax.numpy as jnp
from jax import lax
from jax.experimental import pallas as pl
from jax.experimental.pallas import tpu as pltpu
from jax.sharding import PartitionSpec as P

HD = 128
ROWS = 256
GENOMES = 8
SHORT = 7
WIDE = 512
COLS = 1024
START = -1.0e30
NEVER = -2.0e30
LOG2 = math.log2(math.e) / math.sqrt(HD)
MESH = pl.DeviceIdType.MESH
FAR = (0, 1)
LINES = ((8, 1, True), (9, 3, True), (15, 1, False), (16, 3, False))


def iota(shape, axis):
    return lax.broadcasted_iota(jnp.int32, shape, axis)


def kernel(
    lengths_in, residual, streams, short_in, medium_in, queries, keys, values, w_out,
    hyena, attended, mixed,
    lengths, short, medium, plain, tq, tv, qt, even, odd, kb, vt, gk, mst, lst, acc, oth, ost, ob, att, wb, sums, res, mix,
    taps_ref, sb, f0, prod, hyo, lo_sem,
    a_send, a_recv, g_send, g_recv, h_send, h_recv, z_send, z_recv, r_send, r_recv,
    o_send, o_recv, w_send, w_recv, s_send, s_recv, l_send, l_recv, m_send, m_recv,
    p_send, p_recv, n_send, n_recv,
):
    c, t = lax.axis_index("ctx"), lax.axis_index("tp")
    z, x, y = c // 16, lax.rem(c // 4, 4), lax.rem(c, 4)
    zh, p = t // 2, lax.rem(t, 2)
    a, b = x + (y - x) * p, y + (x - y) * p
    sa, sb_ = 4 - 3 * p, 1 + 3 * p

    def ring(v, d):
        return lax.rem(v + d, 4)

    def dev(a1, b1):
        return (16 * z + a1 * sa + b1 * sb_, t)

    def tile(a1, b1):
        return a1 * sa + b1 * sb_

    left, right = dev(a, ring(b, 3)), dev(a, ring(b, 1))
    across = (lax.rem(c + 16, 32), t)
    sibling = (c, t + 1 - 2 * p)
    after, before = (lax.rem(c + 1, 32), t), (lax.rem(c + 31, 32), t)

    def remote(src, dst, send, recv, to):
        return pltpu.make_async_remote_copy(
            src_ref=src, dst_ref=dst, send_sem=send, recv_sem=recv, device_id=to, device_id_type=MESH
        )

    def head(ref, h):
        return ref.at[:, pl.ds(pl.multiple_of(h * HD, HD), HD)]

    me = tile(a, b)
    both_in = [
        pltpu.make_async_copy(queries, plain.at[0], lo_sem.at[2]),
        pltpu.make_async_copy(values, plain.at[1], lo_sem.at[1]),
    ]
    small_in = [
        pltpu.make_async_copy(lengths_in, lengths, lo_sem.at[13]),
        pltpu.make_async_copy(short_in, short, lo_sem.at[14]),
        pltpu.make_async_copy(medium_in, medium, lo_sem.at[15]),
    ]
    own = pltpu.make_async_copy(head(keys, a), kb.at[me], lo_sem.at[0])
    for copy in both_in + small_in + [own]:
        copy.start()
    streams_in = pltpu.make_async_copy(streams, sb.at[:, pl.ds(16, ROWS)], lo_sem.at[3])
    streams_in.start()
    residual_in = pltpu.make_async_copy(residual, res, lo_sem.at[4])

    def block_cols(j, rows):
        return w_out.at[rows, :, pl.ds(pl.multiple_of(j * COLS, COLS), COLS)]

    every = pl.ds(0, 16)
    weights_in = pltpu.make_async_copy(block_cols(t, every), wb.at[0, p], lo_sem.at[5])
    over_z = [
        (c, lax.rem(2 * zh + 2 * d, 8) + core) for d in (1, 2, 3) for core in range(2)
    ]

    barrier = pltpu.get_barrier_semaphore()
    partners = [dev(ring(a, d), b) for d in (1, 2, 3)] + over_z + [
        left, right, across, sibling, after, before,
    ]
    for to in partners:
        pl.semaphore_signal(barrier, inc=1, device_id=to, device_id_type=MESH)
    for i, copy in enumerate(both_in):
        copy.wait()
        for h in range(4):
            turned = plain[i, :, h * HD : (h + 1) * HD].astype(jnp.float32).T
            (tq, tv)[i][h] = turned.astype(jnp.bfloat16)
    top = pl.ds(0, HD)
    qt[a, 0:HD] = tq[a]
    vt[me] = tv[a]
    pl.semaphore_wait(barrier, len(partners))

    def spread(d, i):
        to_a = ring(a, d)
        src = (head(keys, to_a), tv.at[to_a], tq.at[to_a])[i]
        dst = (kb.at[me], vt.at[me], qt.at[a, top])[i]
        return remote(src, dst, a_send.at[d - 1, i], a_recv.at[d - 1, i], dev(to_a, b))

    def spread_in(d, i):
        from_a = ring(a, 4 - d)
        dst = (kb.at[tile(from_a, b)], vt.at[tile(from_a, b)], qt.at[from_a, top])[i]
        return remote(dst, dst, a_send.at[d - 1, i], a_recv.at[d - 1, i], dev(from_a, b))

    for i in (2, 0, 1):
        for d in (1, 3, 2):
            spread(d, i).start()
    halo = remote(
        streams.at[:, pl.ds(ROWS - 16, 16)], sb.at[:, pl.ds(0, 16)], h_send.at[0], h_recv.at[0], after
    )
    halo.start()
    swap = remote(
        block_cols(t + 1 - 2 * p, every), wb.at[0, p], w_send.at[0], w_recv.at[0], sibling
    )

    def shard(d, core):
        spot = y * 4 + x + (x * 4 + y - y * 4 - x) * core
        to = lax.rem(2 * zh + 2 * d, 8) + core
        return remote(
            block_cols(to, spot), wb.at[4 - d, p, spot],
            s_send.at[d - 1, core], s_recv.at[d - 1, p], (c, to),
        )

    def shard_in(d, core):
        ref = wb.at[4 - d, core, 4 * b + a]
        return remote(ref, ref, s_send.at[d - 1, core], s_recv.at[d - 1, core], sibling)

    for d in (3, 1):
        for core in range(2):
            shard(d, core).start()

    def shards_start():
        for core in range(2):
            shard(2, core).start()
        for copy in (weights_in, swap, residual_in):
            copy.start()

    prev_a, next_a = dev(ring(a, 3), b), dev(ring(a, 1), b)
    pair = pl.ds(0, 2)

    def line(k, op):
        e, here = k, 4 * b
        ref = (
            wb.at[e, pair, here + a], wb.at[e, pair, here + a],
            wb.at[e, 0, here + ring(a, 3)], wb.at[e, 1, here + ring(a, 1)],
        )[op]
        to = next_a if op % 2 == 0 else prev_a
        return remote(ref, ref, l_send.at[k - 1, op], l_recv.at[k - 1, op], to)

    def line_in(k, op):
        e, here = k, 4 * b
        ref = (
            wb.at[e, pair, here + ring(a, 3)], wb.at[e, pair, here + ring(a, 1)],
            wb.at[e, 0, here + ring(a, 2)], wb.at[e, 1, here + ring(a, 2)],
        )[op]
        return remote(ref, ref, l_send.at[k - 1, op], l_recv.at[k - 1, op], next_a)

    def block(k, core, d):
        return wb.at[k, core, pl.ds(4 * ring(b, d), 4)]

    def plane(k, op):
        ref = block(k, (0, 1, 0, 1, 0, 1)[op], (0, 0, 0, 0, 3, 1)[op])
        to = right if op in (0, 1, 4) else left
        return remote(ref, ref, m_send.at[k - 1, op], m_recv.at[k - 1, op], to)

    def plane_in(k, op):
        ref = block(k, (0, 1, 0, 1, 0, 1)[op], (3, 3, 1, 1, 2, 2)[op])
        return remote(ref, ref, m_send.at[k - 1, op], m_recv.at[k - 1, op], left)

    def line_start(k):
        for core in range(2):
            shard_in(4 - k, core).wait_recv()
        line(k, 0).start()
        line(k, 1).start()

    def line_onward(k):
        line_in(k, 0).wait_recv()
        line(k, 2).start()
        line_in(k, 1).wait_recv()
        line(k, 3).start()

    def plane_start(k):
        line_in(k, 2).wait_recv()
        line_in(k, 3).wait_recv()
        for op in (0, 3, 1, 2):
            plane(k, op).start()

    def plane_onward(k):
        plane_in(k, 0).wait_recv()
        plane(k, 4).start()
        plane_in(k, 3).wait_recv()
        plane(k, 5).start()

    def plane_wait(k):
        for op in (1, 2, 4, 5):
            plane_in(k, op).wait_recv()

    def gather(d, i, way):
        j = tile(ring(a, 4 - d), b)
        ref = (kb, vt)[i].at[j]
        to = right if way == 0 else left
        return remote(ref, ref, g_send.at[d, 2 * i + way], g_recv.at[d, 2 * i + way], to)

    def gather_in(d, i, way):
        j = tile(ring(a, 4 - d), ring(b, 3 if way == 0 else 1))
        ref = (kb, vt)[i].at[j]
        return remote(ref, ref, g_send.at[d, 2 * i + way], g_recv.at[d, 2 * i + way], left)

    def onward(d, i):
        j = tile(ring(a, 4 - d), ring(b, 3 if FAR[i] == 0 else 1))
        ref = (kb, vt)[i].at[j]
        to = right if FAR[i] == 0 else left
        return remote(ref, ref, g_send.at[d, 4 + i], g_recv.at[d, 4 + i], to)

    def onward_in(d, i):
        ref = (kb, vt)[i].at[tile(ring(a, 4 - d), ring(b, 2))]
        return remote(ref, ref, g_send.at[d, 4 + i], g_recv.at[d, 4 + i], left)

    def visit(d):
        i = ring(a, 4 - d)
        return remote(qt.at[i, top], qt.at[4 + i, top], z_send.at[d], z_recv.at[d], across)

    def pass_on(d):
        for i in range(2):
            for way in range(2):
                gather(d, i, way).start()

    own.wait()
    pass_on(0)

    @pl.when(z == 1)
    def _():
        visit(0).start()

    for copy in small_in:
        copy.wait()
    starts, ends, total = [], [], jnp.int32(0)
    for j in range(GENOMES):
        starts.append(total)
        total = total + lengths[j]
        ends.append(total)
    def bounds(index):
        low, high = jnp.zeros(index.shape, jnp.int32), jnp.zeros(index.shape, jnp.int32)
        for j in range(GENOMES):
            low = jnp.where(index == j, starts[j], low)
            high = jnp.where(index == j, ends[j], high)
        return low, high

    def inside(position, axis, limits):
        spot = position + iota((ROWS, HD) if axis == 0 else (HD, ROWS), axis)
        return (spot >= limits[0]) & (spot < limits[1])

    by_lane, by_row = bounds(iota((1, HD), 1)), bounds(iota((HD, 1), 0))

    @pl.loop(0, 16)
    def _(j):
        gk[j] = jnp.where(inside((16 * z + j) * ROWS, 0, by_lane), 0.0, NEVER).astype(jnp.bfloat16)

    @pl.loop(0, 8)
    def _(i):
        j = tile(lax.rem(i, 4), b) + 16 * jnp.where(i >= 4, 1, z)
        qt[i, HD:] = jnp.where(inside(j * ROWS, 1, by_row), 1.0, 0.0).astype(jnp.bfloat16)

    mst[...] = jnp.full(mst.shape, START, jnp.float32)
    lst[...] = jnp.zeros(lst.shape, jnp.float32)
    acc[...] = jnp.zeros(acc.shape, jnp.float32)

    for d in (1, 3, 2):
        spread_in(d, 2).wait_recv()

        @pl.when(z == 1)
        def _():
            visit(d).start()

    shards_start()
    for d in (1, 3, 2):
        spread_in(d, 0).wait_recv()
        spread_in(d, 1).wait_recv()
        pass_on(d)

    slots = [tile(i, b) for i in range(4)]

    def fetch(n):
        near, far = (n >= 4) & (n < 12), (n >= 12) & (n < 16)
        d = jnp.where(near, n // 2 - 2, jnp.where(far, n - 12, 0))
        side = jnp.where(near, 3 - 2 * lax.rem(n, 2), jnp.where(far, 2, 0))
        j = step_tile(n)

        @pl.when((z == 0) & (n > 0) & (n < 5))
        def _():
            ref = qt.at[3 + n, top]
            remote(
                ref, ref, z_send.at[0], z_recv.at[ring(a, 5 - n)], across
            ).wait_recv()

        @pl.when(near & (side == 3))
        def _():
            for i in range(2):
                gather_in(d, i, 0).wait_recv()
                if FAR[i] == 0:
                    onward(d, i).start()

        @pl.when(near & (side == 1))
        def _():
            for i in range(2):
                gather_in(d, i, 1).wait_recv()
                if FAR[i] == 1:
                    onward(d, i).start()

        @pl.when(far)
        def _():
            onward_in(d, 0).wait_recv()
            onward_in(d, 1).wait_recv()

        return plan(n, j)

    def plan(n, j):
        same, prior = n == 16, n == 17
        ks = [
            jnp.where(same, slots[i], jnp.where(prior, jnp.maximum(slots[i] - 1, 0), j))
            for i in range(4)
        ]
        ss = [
            jnp.where(
                prior & (slots[i] == 0), 8, i + 4 * jnp.where(same | prior | (j > slots[i]), 1, 0)
            )
            for i in range(4)
        ]
        return j, ks, ss

    def score(k, s, buf, i):
        q = jnp.minimum(s, 7)
        wide_k = jnp.concatenate([kb[k], gk[k]], axis=1)
        buf[i] = jnp.dot(wide_k, qt[q], preferred_element_type=jnp.float32)

    def weigh(k, s, buf, i):
        scores, old = buf[i], mst[s]
        new = jnp.maximum(old, jnp.max(scores, axis=0, keepdims=True))
        exps = jnp.exp2(scores * LOG2 - new[0:1] * LOG2)
        fade = jnp.exp2((old - new) * LOG2)
        mst[s] = new
        lst[s] = lst[s] * fade + jnp.sum(exps.reshape(ROWS // 8, 8, ROWS), axis=0)
        acc[s] = acc[s] * fade[0:1] + jnp.dot(
            vt[k], exps.astype(jnp.bfloat16), preferred_element_type=jnp.float32
        )

    def causal(n, buf):
        @pl.when(n < 4)
        def _():
            ahead = iota((ROWS, ROWS), 0) <= iota((ROWS, ROWS), 1)
            buf[n] = jnp.where(ahead, buf[n], NEVER)

    def step(n, buf, following):
        _, ks_next, ss_next = fetch(jnp.minimum(n + 1, 17))
        for when, k, starts_line in LINES:

            @pl.when(n == when)
            def _():
                (line_start if starts_line else line_onward)(k)

        _, ks, ss = plan(n, step_tile(n))
        for i in range(4):
            score(ks_next[i], ss_next[i], following, i)
            weigh(ks[i], ss[i], buf, i)
        causal(n + 1, following)

    def step_tile(n):
        near, far = (n >= 4) & (n < 12), (n >= 12) & (n < 16)
        d = jnp.where(near, n // 2 - 2, jnp.where(far, n - 12, 0))
        side = jnp.where(near, 3 - 2 * lax.rem(n, 2), jnp.where(far, 2, 0))
        own_line = jnp.where(n < 4, n, 3)
        return tile(jnp.where(near | far, ring(a, 4 - d), own_line), ring(b, side))

    @pl.when(z == 1)
    def _():
        qt[4:8, 0:HD] = jnp.zeros((4, HD, ROWS), jnp.bfloat16)

    _, first_ks, first_ss = plan(jnp.int32(0), tile(0, b))
    for i in range(4):
        score(first_ks[i], first_ss[i], even, i)
    causal(jnp.int32(0), even)

    @pl.loop(0, 9)
    def _(n):
        step(2 * n, even, odd)
        step(2 * n + 1, odd, even)

    def give(i):
        return [
            remote(oth.at[0, i], oth.at[1, i], r_send.at[0, i], r_recv.at[0, i], across),
            remote(ost.at[0, i], ost.at[1, i], r_send.at[1, i], r_recv.at[1, i], across),
        ]

    def close(i):
        total = jnp.sum(lst[i], axis=0, keepdims=True)
        return total, acc[i] * (1.0 / jnp.maximum(total, 1.0e-30))

    base = c * ROWS
    tail = remote(
        prod.at[:, pl.ds(ROWS, 128)], prod.at[:, pl.ds(0, 128)], h_send.at[1], h_recv.at[1], after
    )

    def featurize():
        streams_in.wait()
        halo.wait_recv()
        spot = base + iota((ROWS, HD), 0)
        first = jnp.zeros((ROWS, HD), jnp.int32)
        for j in range(1, GENOMES):
            first = jnp.where(spot >= starts[j], starts[j], first)
        depth = spot - first

        @pl.loop(0, 4)
        def _(n):
            lanes = pl.ds(pl.multiple_of(n * HD, HD), HD)
            made = []
            for j in range(3):
                data = sb[j, :, lanes].astype(jnp.float32)
                taps = short[j, :, lanes].astype(jnp.float32)
                total = data[16:] * taps[0:1]
                for lag in range(1, SHORT):
                    moved = pltpu.roll(data, lag, 0)[16:]
                    total = total + jnp.where(depth >= lag, moved * taps[lag : lag + 1], 0.0)
                made.append(total.astype(jnp.bfloat16))
            f0[n] = made[0]
            prod[n, pl.ds(128, ROWS)] = (
                made[1].astype(jnp.float32) * made[2].astype(jnp.float32)
            ).astype(jnp.bfloat16)
        tail.start()

    def spread_weights():
        line_start(2)
        for k in (1, 3):
            plane_start(k)

    def chores():
        spread_weights()
        featurize()
        line_onward(2)

    def home(d):
        to_a = ring(a, d)
        return remote(ob.at[to_a], att.at[0, p, a], o_send.at[d - 1], o_recv.at[d - 1], dev(to_a, b))

    def home_in(d):
        ref = att.at[0, p, ring(a, 4 - d)]
        return remote(ref, ref, o_send.at[d - 1], o_recv.at[d - 1], dev(ring(a, 4 - d), b))

    @pl.when(z == 1)
    def _():
        chores()
        plane_onward(1)

    for d in (1, 2, 3, 0):
        i = ring(a, d)
        total, out = close(i)
        ob[i] = out.T.astype(jnp.bfloat16)

        @pl.when(z == 1)
        def _():
            for copy in give(i):
                copy.wait_recv()
            m_other, l_other = ost[1, i, 0, 0:1], ost[1, i, 1, 0:1]
            m_own = mst[i, 0:1]
            top = jnp.maximum(m_own, m_other)
            w_own = jnp.exp2((m_own - top) * LOG2) * total
            w_other = jnp.exp2((m_other - top) * LOG2) * l_other
            share = 1.0 / (w_own + w_other)
            both = out * (w_own * share) + oth[1, i].astype(jnp.float32) * (w_other * share)
            ob[i] = both.T.astype(jnp.bfloat16)

        if d > 0:
            home(d).start()
        else:
            att[0, p, a] = ob[i]

    up, down = (c, lax.rem(t + 2, 8)), (c, lax.rem(t + 6, 8))
    halves = (pl.ds(0, 2), pl.ds(2, 2))

    def climb(op):
        half = (0, 1, 0, 1, 0, 1)[op]
        src = (0, 0, 0, 0, 3, 1)[op]
        dst = (3, 3, 1, 1, 2, 2)[op]
        to = up if op in (0, 1, 4) else down
        return remote(
            att.at[src, p, halves[half]], att.at[dst, p, halves[half]],
            p_send.at[op], p_recv.at[op], to,
        )

    def climb_in(op):
        ref = att.at[(3, 3, 1, 1, 2, 2)[op], p, halves[op % 2]]
        return remote(ref, ref, p_send.at[op], p_recv.at[op], up)

    def cross(op):
        ref = att.at[0, p] if op == 6 else att.at[(3, 3, 1, 1, 2, 2)[op], p, halves[op % 2]]
        return remote(ref, ref, n_send.at[op], n_recv.at[op], sibling)

    def cross_in(op):
        q = 1 - p
        ref = att.at[0, q] if op == 6 else att.at[(3, 3, 1, 1, 2, 2)[op], q, halves[op % 2]]
        return remote(ref, ref, n_send.at[op], n_recv.at[op], sibling)

    def multiply(e):
        rows = jnp.concatenate([att[e, core, i] for core in range(2) for i in range(4)], axis=1)

        @pl.loop(0, 2)
        def _(n):
            lanes = pl.ds(pl.multiple_of(n * 512, 512), 512)
            w = wb[e, :, :, :, lanes].reshape(1024, 512)
            sums[:, lanes] += jnp.dot(rows, w, preferred_element_type=jnp.float32)

    flip = jnp.where(
        lax.rem(iota((128, 128), 0) + iota((128, 128), 1), 128) == 0, 1.0, 0.0
    ).astype(jnp.bfloat16)
    taps_back = jnp.dot(medium[...], flip, preferred_element_type=jnp.float32)
    hyo_taps = taps_back

    def genome_at(position):
        genome = jnp.zeros(position.shape, jnp.int32)
        for j in range(GENOMES):
            genome = genome + jnp.where(position >= ends[j], 1, 0)
        return genome

    taps_ref[...] = hyo_taps.reshape(4, 8, 128)

    def convolve(n):
        lt, blk = n // 2, lax.rem(n, 2)
        here = base + blk * 128
        rows, cols = iota((128, 128), 0), iota((128, 128), 1)
        genome_now = genome_at(here + rows)
        genome_src = genome_at(here + cols)
        earlier = here - 128 + cols
        genome_prev = genome_at(earlier)
        near = (genome_now == genome_src) & (rows >= cols)
        far = (genome_now == genome_prev) & (rows < cols) & (earlier >= 0)
        data = prod[lt, pl.ds(pl.multiple_of(blk * 128, 128), 256)]
        band = iota((128, 128), 1) // 16
        out = jnp.zeros((128, 128), jnp.float32)
        for g in range(8):
            taps = jnp.broadcast_to(taps_ref[lt, g : g + 1], (128, 128))
            around = pltpu.roll(taps, 0, 1, stride=1, stride_axis=0)
            weights = jnp.concatenate(
                [jnp.where(far, around, 0.0), jnp.where(near, around, 0.0)], axis=1
            ).astype(jnp.bfloat16)
            term = jnp.dot(weights, data, preferred_element_type=jnp.float32)
            out = jnp.where(band == g, term, out)
        place = pl.ds(pl.multiple_of(blk * 128, 128), 128)
        hyo[lt, place] = (f0[lt, place].astype(jnp.float32) * out).astype(jnp.bfloat16)

    @pl.when(z == 0)
    def _():
        for i in range(4):
            total, out = close(4 + i)
            oth[0, i] = out.astype(jnp.bfloat16)
            ost[0, i, 0] = mst[4 + i]
            ost[0, i, 1] = jnp.broadcast_to(total, (8, ROWS))
            for copy in give(i):
                copy.start()

    @pl.when(z == 0)
    def _():
        chores()

    for d in (1, 2, 3):
        home_in(d).wait_recv()
    for op in (0, 3):
        climb(op).start()
    cross(6).start()
    attended_out = [
        pltpu.make_async_copy(att.at[0, p, i], head(attended, i), lo_sem.at[6 + i]) for i in range(4)
    ]
    for copy in attended_out:
        copy.start()
    residual_in.wait()
    sums[...] = res[...].astype(jnp.float32)
    @pl.when(z == 0)
    def _():
        plane_onward(1)

    plane_start(2)
    tail.wait_recv()

    @pl.loop(0, 4)
    def _(n):
        convolve(n)

    for op in (1, 2):
        climb(op).start()
    plane_onward(3)
    climb_in(0).wait_recv()
    climb(4).start()
    cross(0).start()
    climb_in(3).wait_recv()
    climb(5).start()
    cross(3).start()

    plane_onward(2)

    @pl.loop(4, 8)
    def _(n):
        convolve(n)

    hyena_out = [
        pltpu.make_async_copy(hyo.at[i], head(hyena, i), lo_sem.at[i]) for i in range(4)
    ]
    for copy in hyena_out:
        copy.start()
    for op in (1, 2):
        climb_in(op).wait_recv()
        cross(op).start()
    weights_in.wait()
    cross_in(6).wait_recv()
    remote(wb.at[0, 1 - p], wb.at[0, 1 - p], w_send.at[0], w_recv.at[0], sibling).wait_recv()
    multiply(0)
    for d in (1, 2, 3):
        for i in range(3):
            spread(d, i).wait_send()
        home(d).wait_send()
        for core in range(2):
            shard(d, core).wait_send()
        for op in range(4):
            line(d, op).wait_send()
    halo.wait_send()
    tail.wait_send()
    swap.wait_send()
    for d in range(4):
        for i in range(2):
            for way in range(2):
                gather(d, i, way).wait_send()
            onward(d, i).wait_send()

    @pl.when(z == 1)
    def _():
        for d in range(4):
            visit(d).wait_send()

    @pl.when(z == 0)
    def _():
        for i in range(4):
            for copy in give(i):
                copy.wait_send()

    for copy in hyena_out + attended_out:
        copy.wait()
    for e, ops in ((1, (2, 3)), (3, (0, 1)), (2, (4, 5))):
        plane_wait(e)
        for op in ops:
            cross_in(op).wait_recv()
        if e == 1:
            for op in (4, 5):
                climb_in(op).wait_recv()
                cross(op).start()
        if e != 2:
            multiply(e)
    rows = jnp.concatenate([att[2, core, i] for core in range(2) for i in range(4)], axis=1)
    mixed_out = []
    for n in range(4):
        lanes = slice(n * 256, (n + 1) * 256)
        w = wb[2, :, :, :, lanes].reshape(1024, 256)
        mix[:, lanes] = (
            sums[:, lanes] + jnp.dot(rows, w, preferred_element_type=jnp.float32)
        ).astype(jnp.bfloat16)
        for m in range(2):
            place = (pl.ds(m * 128, 128), lanes)
            mixed_out.append(
                pltpu.make_async_copy(mix.at[place], mixed.at[place], lo_sem.at[(4, 5, 13, 14, 15, 10, 11, 12)[2 * n + m]])
            )
            mixed_out[-1].start()

    for d in (1, 2, 3):
        for op in range(6):
            plane(d, op).wait_send()
    for op in range(6):
        climb(op).wait_send()
    for op in range(7):
        cross(op).wait_send()
    for copy in mixed_out:
        copy.wait()


def hand_out(a_in, b_in, c_in, a_out, b_out, c_out, a_mid, b_mid, c_mid, sem):
    parts = [
        (src.at[rows], mid.at[rows], dst.at[rows], sem.at[n, i])
        for n, (src, mid, dst) in enumerate(
            ((a_in, a_mid, a_out), (b_in, b_mid, b_out), (c_in, c_mid, c_out))
        )
        for i, rows in enumerate((pl.ds(0, 128), pl.ds(128, 128)))
    ]
    first = [pltpu.make_async_copy(src, mid, s.at[0]) for src, mid, _, s in parts]
    second = [pltpu.make_async_copy(mid, dst, s.at[1]) for _, mid, dst, s in parts]
    for copy in first:
        copy.start()
    for one, two in zip(first, second):
        one.wait()
        two.start()
    for copy in second:
        copy.wait()


def body(residual, streams, short_filter, medium_filter, queries, keys, values, lengths, w_out):
    bf16, f32 = jnp.bfloat16, jnp.float32
    anywhere = pl.BlockSpec(memory_space=pl.ANY)
    dma = pltpu.SemaphoreType.DMA
    scratch = [
        pltpu.SMEM((GENOMES,), jnp.int32),
        pltpu.VMEM((3, SHORT, 512), bf16),
        pltpu.VMEM((32, 128), bf16),
        pltpu.VMEM((2, ROWS, 512), bf16),
        pltpu.VMEM((4, HD, ROWS), bf16),
        pltpu.VMEM((4, HD, ROWS), bf16),
        pltpu.VMEM((8, 2 * HD, ROWS), bf16),
        pltpu.VMEM((4, ROWS, ROWS), f32),
        pltpu.VMEM((4, ROWS, ROWS), f32),
        pltpu.VMEM((16, ROWS, HD), bf16),
        pltpu.VMEM((16, HD, ROWS), bf16),
        pltpu.VMEM((16, ROWS, HD), bf16),
        pltpu.VMEM((9, 8, ROWS), f32),
        pltpu.VMEM((9, 8, ROWS), f32),
        pltpu.VMEM((9, HD, ROWS), f32),
        pltpu.VMEM((2, 4, HD, ROWS), bf16),
        pltpu.VMEM((2, 4, 2, 8, ROWS), f32),
        pltpu.VMEM((4, ROWS, HD), bf16),
        pltpu.VMEM((4, 2, 4, ROWS, HD), bf16),
        pltpu.VMEM((4, 2, 16, 32, COLS), bf16),
        pltpu.VMEM((ROWS, COLS), f32),
        pltpu.VMEM((ROWS, COLS), bf16),
        pltpu.VMEM((ROWS, COLS), bf16),
        pltpu.VMEM((4, 8, 128), f32),
        pltpu.VMEM((3, ROWS + 16, 512), bf16),
        pltpu.VMEM((4, ROWS, HD), bf16),
        pltpu.VMEM((4, ROWS + 128, HD), bf16),
        pltpu.VMEM((4, ROWS, HD), bf16),
        dma((16,)),
        dma((3, 3)), dma((3, 3)),
        dma((4, 6)), dma((4, 6)),
        dma((2,)), dma((2,)),
        dma((4,)), dma((4,)),
        dma((2, 4)), dma((2, 4)),
        dma((4,)), dma((4,)),
        dma((1,)), dma((1,)),
        dma((3, 2)), dma((3, 2)),
        dma((3, 4)), dma((3, 4)),
        dma((3, 6)), dma((3, 6)),
        dma((6,)), dma((6,)),
        dma((7,)), dma((7,)),
    ]
    made = pl.pallas_call(
        kernel,
        out_shape=(
            jax.ShapeDtypeStruct((ROWS, 512), bf16),
            jax.ShapeDtypeStruct((ROWS, 512), bf16),
            jax.ShapeDtypeStruct((ROWS, COLS), bf16),
        ),
        in_specs=[anywhere] * 9,
        out_specs=(anywhere, anywhere, anywhere),
        scratch_shapes=scratch,
        compiler_params=pltpu.CompilerParams(
            collective_id=0, has_side_effects=True, vmem_limit_bytes=56 * 1024 * 1024
        ),
        cost_estimate=pl.CostEstimate(
            flops=7_000_000_000, bytes_accessed=16_000_000, transcendentals=5_000_000
        ),
        name="mixer",
    )(
        lengths, residual, jnp.transpose(streams, (1, 0, 2)), jnp.transpose(short_filter, (1, 0, 2)),
        medium_filter.T, queries, keys, values, w_out.reshape(16, 32, 8192),
    )
    return pl.pallas_call(
        hand_out,
        out_shape=tuple(jax.ShapeDtypeStruct(v.shape, v.dtype) for v in made),
        in_specs=[anywhere] * 3,
        out_specs=(anywhere,) * 3,
        scratch_shapes=[pltpu.VMEM(v.shape, v.dtype) for v in made] + [dma((3, 2, 2))],
        name="hand_out",
    )(*made)


def solution(mesh):
    in_specs = (
        P("ctx", "tp"),
        P("ctx", None, "tp"),
        P(None, None, "tp"),
        P(None, "tp"),
        P("ctx", "tp"),
        P("ctx", "tp"),
        P("ctx", "tp"),
        P(),
        P("tp", None),
    )
    out_specs = (P("ctx", "tp"), P("ctx", "tp"), P("ctx", "tp"))
    return jax.shard_map(body, mesh=mesh, in_specs=in_specs, out_specs=out_specs, check_vma=False)
```
